256 devices in a mesh: seq: 16 (over z_lo, y, core), mlp: 16 (over x, z_hi).
Axes of the slice: x: 4, y: 4, z: 8 (z_hi: 4, z_lo: 2; z = z_hi * 2 + z_lo), core: 2. Of those that a mesh axis runs over, the one named last changes fastest.
Arguments:
- txt_q: bfloat16 [512, 2048], replicated, may hold values from -6 to 6
- txt_k: bfloat16 [512, 2048], replicated, may hold values from -6 to 6
- txt_v: bfloat16 [512, 2048], replicated, may hold values from -6 to 6
- txt_grad: bfloat16 [512, 2048], replicated, may hold values from -6 to 6
- img_q: bfloat16 [4096, 2048], P(('seq', 'mlp')), may hold values from -300 to 300
- img_k: bfloat16 [4096, 2048], P(('seq', 'mlp')), may hold values from -6 to 6
- img_v: bfloat16 [4096, 2048], P(('seq', 'mlp')), may hold values from -6 to 6
- img_grad: bfloat16 [4096, 2048], P(('seq', 'mlp')), may hold values from -6 to 6
Outputs:
- img_dq: float32 [4096, 2048], P(('seq', 'mlp'))
- img_dk: float32 [4096, 2048], P(('seq', 'mlp'))
- img_dv: float32 [4096, 2048], P(('seq', 'mlp'))
- txt_dq: float32 [512, 2048], P('mlp', 'seq')
- txt_dk: float32 [512, 2048], P('mlp', 'seq')
- txt_dv: float32 [512, 2048], P('mlp', 'seq')
The draws below stay inside these ranges and needn't reach their ends.
All inputs are finite; a program needn't handle non-finite values.
Results may differ from the reference program's by a relative error of at most 0.014.
Values may be sent and summed in bfloat16 or wider, within the bound.
A program may use at most 128 MiB of HBM per device.

```python
import math
import jax
import jax.numpy as jnp
from jax import lax

HD = 128
HEADS = 16
D_ATT = 2048
TXT = 512
IMG = 4096


def shared_keys(key):
    return jnp.clip(jax.random.normal(key, (IMG, HEADS * HD), jnp.float32), -6.0, 6.0)


def draw_img_k(key, part):
    base = shared_keys(key)
    return base.astype(jnp.bfloat16)


def draw_img_q(key, part):
    key = jax.random.fold_in(key, 5)
    fresh_key = jax.random.fold_in(key, 0)
    fresh = jnp.clip(jax.random.normal(fresh_key, (IMG, HEADS * HD), jnp.float32), -6.0, 6.0)
    return fresh.astype(jnp.bfloat16)


def levels(rng, dims, cuts, low, high):
    def one(dim, shards_of):
        heights = jax.random.uniform(jax.random.fold_in(jax.random.fold_in(rng, 6), dim), (shards_of,), jnp.float32, low / len(cuts), high / len(cuts))
        return jnp.repeat(jnp.exp(heights), dims[dim] // shards_of).reshape((-1,) + (1,) * (len(dims) - dim - 1))

    gain = one(*cuts[0])
    for cut in cuts[1:]:
        gain = gain * one(*cut)
    return gain


def scatter_about(stream_key, dims, spread, limit, shards=(), kind=jnp.bfloat16):
    factor_of = levels(stream_key, dims, shards, -0.22, 0.18) if shards else 1.0
    values = jax.random.normal(stream_key, dims, jnp.float32) * spread * factor_of
    return jnp.minimum(jnp.maximum(values, -limit), limit).astype(kind)


def setup_inputs(seed: int = 0) -> dict:
    splits = jax.random.split(jax.random.key(seed), 9)
    return {
        "txt_q": scatter_about(splits[0], (TXT, D_ATT), 1.0, 6.0),
        "txt_k": scatter_about(splits[1], (TXT, D_ATT), 1.0, 6.0),
        "txt_v": scatter_about(splits[2], (TXT, D_ATT), 1.0, 6.0),
        "txt_grad": scatter_about(splits[3], (TXT, D_ATT), 1.0, 6.0),
        "img_q": draw_img_q(jax.random.fold_in(splits[8], 71), 0),
        "img_k": draw_img_k(jax.random.fold_in(splits[8], 71), 0),
        "img_v": scatter_about(splits[6], (IMG, D_ATT), 1.0, 6.0, ((0, 256),)),
        "img_grad": scatter_about(splits[7], (IMG, D_ATT), 1.0, 6.0, ((0, 256),)),
    }


def attend_block(queries, cotangent, all_keys, values, score_scale):
    queries = queries.astype(jnp.float32)
    cotangent = cotangent.astype(jnp.float32)
    key_block = all_keys.astype(jnp.float32)
    value_block = values.astype(jnp.float32)
    scores = jnp.einsum("qd,kd->qk", queries, key_block) * score_scale
    weights = jnp.exp(scores - jnp.max(scores, axis=1, keepdims=True))
    weights = weights / jnp.sum(weights, axis=1, keepdims=True)
    rounded = weights.astype(jnp.bfloat16).astype(jnp.float32)
    dprob = jnp.einsum("qd,kd->qk", cotangent, value_block)
    delta = jnp.sum(weights * dprob, axis=1, keepdims=True)
    dscore = (weights * (dprob - delta)).astype(jnp.bfloat16).astype(jnp.float32)
    d_query = jnp.einsum("qk,kd->qd", dscore, key_block) * score_scale
    d_key = jnp.einsum("qk,qd->kd", dscore, queries) * score_scale
    d_value = jnp.einsum("qk,qd->kd", rounded, cotangent)
    return d_query, jnp.concatenate([d_key, d_value], axis=1)


def reference(txt_q, txt_k, txt_v, txt_grad, img_q, img_k, img_v, img_grad):
    total_rows = TXT + IMG
    block_rows = math.gcd(total_rows, 512)
    score_scale = HD ** -0.5

    def heads_first(text_part, image_part):
        joined = jnp.concatenate([text_part, image_part], axis=0)
        return joined.reshape(total_rows, HEADS, HD).transpose(1, 0, 2)

    stacked = (heads_first(txt_q, img_q), heads_first(txt_k, img_k), heads_first(txt_v, img_v), heads_first(txt_grad, img_grad))

    def one_head(operands):
        queries, all_keys, values, cotangent = operands

        def visit(carry, block_index):
            row_start = (block_index * block_rows).astype(jnp.int32)
            query_rows = lax.dynamic_slice_in_dim(queries, row_start, block_rows, 0)
            cot_rows = lax.dynamic_slice_in_dim(cotangent, row_start, block_rows, 0)
            d_query, term = attend_block(query_rows, cot_rows, all_keys, values, score_scale)
            return carry + term, d_query

        key_terms, d_query = lax.scan(visit, jnp.zeros((total_rows, 2 * HD), jnp.float32), jnp.arange(total_rows // block_rows, dtype=jnp.int32))
        return d_query.reshape(total_rows, HD), key_terms

    d_query, key_terms = lax.map(one_head, stacked)

    def tokens_first(array):
        return array.transpose(1, 0, 2).reshape(total_rows, HEADS * HD)

    grad_q = tokens_first(d_query)
    grad_k = tokens_first(key_terms[:, :, :HD])
    grad_v = tokens_first(key_terms[:, :, HD:])
    return grad_q[TXT:], grad_k[TXT:], grad_v[TXT:], grad_q[:TXT], grad_k[:TXT], grad_v[:TXT]
```

```python
import jax
import jax.numpy as jnp
from jax import lax
from jax.experimental import pallas as pl
from jax.experimental.pallas import tpu as pltpu
from jax.sharding import PartitionSpec as P

HD = 128
LOG2E = 1.4426950408889634
SCALE = HD ** -0.5
BF = jnp.bfloat16
F32 = jnp.float32
MESH = pl.DeviceIdType.MESH

START = (0, 128, 384, 640, 896)
SIZE = (128, 256, 256, 256, 256)
ROWS = 1152


def nt(a, b):
    return lax.dot_general(a, b, (((1,), (1,)), ((), ())), preferred_element_type=F32)


def nn(a, b):
    return lax.dot_general(a, b, (((1,), (0,)), ((), ())), preferred_element_type=F32)


def body(
    tq, tk, tv, tg, iq, ik, iv, ig,
    oq, ok, ov, otq, otk, otv,
    flat, stage, own, qg, kv, text,
    qall, kall, vall, gall, ktall,
    e_buf, dp_buf, pb_buf, ds_buf, mx, sm, dl, st, st_in,
    dkv_st, dkv_in, dkvt_st, dkvt_in, dkv_own, dkvt_own,
    dq_st, dq_in, dqt_st, dqt_in, dq_own, dqt_own, dq_text,
    out_st, fin, tout, tfin,
    in_sem, text_sem,
    p1_s, p1_r, qg_s, qg_r, kv_s, kv_r, st_s, st_r,
    dkv_s, dkv_r, dkvt_s, dkvt_r, dq_s, dq_r, dqt_s, dqt_r,
    p4_s, p4_r, tx_s, tx_r,
):
    s = lax.axis_index("seq")
    m = lax.axis_index("mlp")
    z0, y, core = s // 8, (s // 2) % 4, s % 2
    x, zh = m // 4, m % 4

    def flip(j):
        zf = 1 - z0 if j & 2 else z0
        cf = 1 - core if j & 1 else core
        return zf * 8 + y * 2 + cf

    def turn(j):
        return z0 * 8 + ((y + j) % 4) * 2 + core

    def around(i, sign):
        dz, dx = i // 4, i % 4
        return ((x + sign * dx + 4) % 4) * 4 + (zh + sign * dz + 4) % 4

    loads = []
    for n, ref in enumerate((iq, ig, ik, iv)):
        c = pltpu.make_async_copy(ref, flat.at[n], in_sem.at[n])
        c.start()
        loads.append(c)
    col = pl.ds(pl.multiple_of(m * HD, HD), HD)
    tloads = []
    for n, ref in enumerate((tq, tg, tk, tv)):
        for j in range(4):
            owner = (j // 2) * 8 + y * 2 + j % 2 if n < 2 else turn((4 - j) % 4)
            rows = pl.ds(pl.multiple_of(owner * 32, 32), 32)
            c = pltpu.make_async_copy(ref.at[rows, col], text.at[n, pl.ds(j * 32, 32)], text_sem.at[n, j])
            c.start()
            tloads.append(c)

    barrier = pltpu.get_barrier_semaphore()
    for j in range(1, 4):
        pl.semaphore_signal(barrier, inc=1, device_id={"seq": flip(j), "mlp": m}, device_id_type=MESH)
        pl.semaphore_signal(barrier, inc=1, device_id={"seq": turn(j), "mlp": m}, device_id_type=MESH)
    for i in range(1, 16):
        pl.semaphore_signal(barrier, inc=1, device_id={"seq": s, "mlp": around(i, 1)}, device_id_type=MESH)

    @pl.when(s != m)
    def _():
        pl.semaphore_signal(barrier, inc=1, device_id={"seq": m, "mlp": s}, device_id_type=MESH)
        pl.semaphore_wait(barrier, 22)

    @pl.when(s == m)
    def _():
        pl.semaphore_wait(barrier, 21)

    for c in loads:
        c.wait()
    for h in range(16):
        for n in range(4):
            stage[h, n] = flat[n, :, h * HD:(h + 1) * HD]

    sends = []
    for i in (8, 9, 11, 10, 4, 12, 5, 13, 7, 15, 6, 14, 1, 3, 2):
        dest = around(i, -1)
        c = pltpu.make_async_remote_copy(
            stage.at[dest], own.at[i], p1_s.at[i], p1_r.at[i],
            device_id={"seq": s, "mlp": dest}, device_id_type=MESH)
        c.start()
        sends.append(c)
    own[0] = stage[m]

    for c in tloads:
        c.wait()
    qall[0:128] = text[0]
    gall[0:128] = text[1]
    kall[0:128] = text[2]
    vall[0:128] = text[3]

    for g in range(4):
        for i in range(4 * g, 4 * g + 4):
            if i:
                pltpu.make_async_copy(own.at[i], own.at[i], p1_r.at[i]).wait()
        part = pl.ds(4 * g, 4)
        for j in (2, 3, 1):
            c = pltpu.make_async_remote_copy(
                own.at[part, pl.ds(0, 2)], qg.at[j - 1, part], qg_s.at[g, j - 1], qg_r.at[g, j - 1],
                device_id={"seq": flip(j), "mlp": m}, device_id_type=MESH)
            c.start()
            sends.append(c)
        for j in (2, 1, 3):
            c = pltpu.make_async_remote_copy(
                own.at[part, pl.ds(2, 2)], kv.at[j - 1, part], kv_s.at[g, j - 1], kv_r.at[g, j - 1],
                device_id={"seq": turn(j), "mlp": m}, device_id_type=MESH)
            c.start()
            sends.append(c)

    qall[128:384] = own[:, 0].reshape(256, HD)
    gall[128:384] = own[:, 1].reshape(256, HD)
    kall[128:384] = own[:, 2].reshape(256, HD)
    vall[128:384] = own[:, 3].reshape(256, HD)

    def pass_one(kc, qc):
        kr, qr = pl.ds(START[kc], SIZE[kc]), pl.ds(START[qc], SIZE[qc])
        scores = nt(kall[kr], qall[qr])
        top = jnp.max(scores, axis=0, keepdims=True)
        e = jnp.exp2((scores - top) * (SCALE * LOG2E))
        dp = nt(vall[kr], gall[qr])
        mx[kc:kc + 1, qr] = top
        sm[kc:kc + 1, qr] = jnp.sum(e, axis=0, keepdims=True)
        dl[kc:kc + 1, qr] = jnp.sum(e * dp, axis=0, keepdims=True)
        e_buf[kr, qr] = e
        dp_buf[kr, qr] = dp

    have_k, have_q = [0, 1], [0, 1]
    for kc in have_k:
        for qc in have_q:
            pass_one(kc, qc)
    for kind, j in (("q", 1), ("k", 1), ("k", 3), ("q", 2), ("k", 2), ("q", 3)):
        r = pl.ds(START[j + 1], 256)
        sem, buf, left, right = (qg_r, qg, qall, gall) if kind == "q" else (kv_r, kv, kall, vall)
        for g in range(4):
            piece = buf.at[j - 1, pl.ds(4 * g, 4)]
            pltpu.make_async_copy(piece, piece, sem.at[g, j - 1]).wait()
        left[r] = buf[j - 1, :, 0].reshape(256, HD)
        right[r] = buf[j - 1, :, 1].reshape(256, HD)
        if kind == "q":
            for kc in have_k:
                pass_one(kc, j + 1)
            have_q.append(j + 1)
        else:
            for qc in have_q:
                pass_one(j + 1, qc)
            have_k.append(j + 1)

    unit = SCALE * LOG2E
    top = jnp.max(mx[0:5], axis=0, keepdims=True)
    w = jnp.exp2((mx[0:5] - top) * unit)
    total = jnp.sum(w * sm[0:5], axis=0, keepdims=True)
    dsum = jnp.sum(w * dl[0:5], axis=0, keepdims=True)
    for b in range(9):
        cols = slice(b * 128, (b + 1) * 128)
        st[b:b + 1] = top[:, cols]
        st[9 + b:10 + b] = total[:, cols]
        st[18 + b:19 + b] = dsum[:, cols]
    for j in (2, 3, 1):
        c = pltpu.make_async_remote_copy(
            st, st_in.at[j - 1], st_s.at[j - 1], st_r.at[j - 1],
            device_id={"seq": flip(j), "mlp": m}, device_id_type=MESH)
        c.start()
        sends.append(c)
    ktall[...] = kall[...].T
    for j in (1, 2, 3):
        pltpu.make_async_copy(st_in.at[j - 1], st_in.at[j - 1], st_r.at[j - 1]).wait()

    def theirs(j, first):
        rows = [0] + [1 + 2 * (r ^ j) + half for r in range(4) for half in range(2)]
        return jnp.concatenate([st_in[j - 1, first + b:first + b + 1] for b in rows], axis=0)

    tops = [st[0:9]] + [theirs(j, 0) for j in (1, 2, 3)]
    sums = [st[9:18]] + [theirs(j, 9) for j in (1, 2, 3)]
    dsums = [st[18:27]] + [theirs(j, 18) for j in (1, 2, 3)]
    gtop = jnp.maximum(jnp.maximum(tops[0], tops[1]), jnp.maximum(tops[2], tops[3]))
    ws = [jnp.exp2((t - gtop) * unit) for t in tops]
    gsum = ws[0] * sums[0] + ws[1] * sums[1] + ws[2] * sums[2] + ws[3] * sums[3]
    gd = ws[0] * dsums[0] + ws[1] * dsums[1] + ws[2] * dsums[2] + ws[3] * dsums[3]
    inv = 1.0 / gsum
    delta = gd * inv

    def as_row(a):
        return jnp.concatenate([a[b:b + 1] for b in range(9)], axis=1)

    gtop_row, inv_row, delta_row = as_row(gtop), as_row(inv), as_row(delta)
    mx[0:5] = jnp.exp2((mx[0:5] - gtop_row) * unit) * inv_row
    dl[0:1] = delta_row

    for kc in (3, 2, 4, 0, 1):
        kr = pl.ds(START[kc], SIZE[kc])
        for qc in range(5):
            qr = pl.ds(START[qc], SIZE[qc])
            p = e_buf[kr, qr] * mx[kc:kc + 1, qr]
            pb_buf[kr, qr] = p.astype(BF)
            ds_buf[kr, qr] = (p * (dp_buf[kr, qr] - dl[0:1, qr])).astype(BF)
        dk = nn(ds_buf[kr], qall[...]) * SCALE
        dv = nn(pb_buf[kr], gall[...])
        if kc >= 2:
            j = kc - 1
            dkv_st[j - 1, 0] = dk.astype(BF)
            dkv_st[j - 1, 1] = dv.astype(BF)
            c = pltpu.make_async_remote_copy(
                dkv_st.at[j - 1], dkv_in.at[j - 1], dkv_s.at[j - 1], dkv_r.at[j - 1],
                device_id={"seq": turn(4 - j), "mlp": m}, device_id_type=MESH)
            c.start()
            sends.append(c)
        elif kc == 0:
            for j in range(4):
                part = slice(j * 32, j * 32 + 32)
                if j == 0:
                    dkvt_own[0] = dk[part]
                    dkvt_own[1] = dv[part]
                else:
                    dkvt_st[j - 1, 0] = dk[part].astype(BF)
                    dkvt_st[j - 1, 1] = dv[part].astype(BF)
                    c = pltpu.make_async_remote_copy(
                        dkvt_st.at[j - 1], dkvt_in.at[j - 1], dkvt_s.at[j - 1], dkvt_r.at[j - 1],
                        device_id={"seq": turn(4 - j), "mlp": m}, device_id_type=MESH)
                    c.start()
                    sends.append(c)
        else:
            dkv_own[0] = dk
            dkv_own[1] = dv

    for qc in (3, 4, 2, 0, 1):
        qr = pl.ds(START[qc], SIZE[qc])
        dqt = nn(ktall[...], ds_buf[:, qr]) * SCALE
        if qc >= 2:
            j = qc - 1
            dq_st[j - 1] = dqt.astype(BF)
            c = pltpu.make_async_remote_copy(
                dq_st.at[j - 1], dq_in.at[j - 1], dq_s.at[j - 1], dq_r.at[j - 1],
                device_id={"seq": flip(j), "mlp": m}, device_id_type=MESH)
            c.start()
            sends.append(c)
        elif qc == 0:
            dq_text[...] = dqt.T
            for j in range(4):
                peer = flip(j)
                part = pl.ds(pl.multiple_of((peer // 8 * 2 + peer % 2) * 32, 32), 32)
                if j == 0:
                    dqt_own[...] = dq_text[part]
                else:
                    dqt_st[j - 1] = dq_text[part].astype(BF)
                    c = pltpu.make_async_remote_copy(
                        dqt_st.at[j - 1], dqt_in.at[j - 1], dqt_s.at[j - 1], dqt_r.at[j - 1],
                        device_id={"seq": flip(j), "mlp": m}, device_id_type=MESH)
                    c.start()
                    sends.append(c)
        else:
            dq_own[...] = dqt

    def arrived(buf, sem):
        for j in range(3):
            pltpu.make_async_copy(buf.at[j], buf.at[j], sem.at[j]).wait()

    def plus(own_term, buf, *at):
        t = own_term
        for j in range(3):
            t = t + buf[(j, *at)].astype(F32)
        return t

    arrived(dkv_in, dkv_r)
    out_st[:, 1] = plus(dkv_own[0], dkv_in, 0).astype(BF).reshape(16, 16, HD)
    out_st[:, 2] = plus(dkv_own[1], dkv_in, 1).astype(BF).reshape(16, 16, HD)
    arrived(dq_in, dq_r)
    out_st[:, 0] = plus(dq_own[...], dq_in).T.astype(BF).reshape(16, 16, HD)
    for i in (8, 9, 11, 10, 4, 12, 5, 13, 7, 15, 6, 14, 1, 3, 2):
        dest = around(i, 1)
        c = pltpu.make_async_remote_copy(
            out_st.at[i], fin.at[m], p4_s.at[i], p4_r.at[i],
            device_id={"seq": s, "mlp": dest}, device_id_type=MESH)
        c.start()
        sends.append(c)
    fin[m] = out_st[0]

    arrived(dkvt_in, dkvt_r)
    arrived(dqt_in, dqt_r)
    tout[0] = plus(dqt_own[...], dqt_in).astype(BF)
    tout[1] = plus(dkvt_own[0], dkvt_in, 0).astype(BF)
    tout[2] = plus(dkvt_own[1], dkvt_in, 1).astype(BF)

    @pl.when(s != m)
    def _():
        c = pltpu.make_async_remote_copy(
            tout, tfin, tx_s, tx_r, device_id={"seq": m, "mlp": s}, device_id_type=MESH)
        c.start()
        c.wait()

    @pl.when(s == m)
    def _():
        tfin[...] = tout[...]

    otq[...] = tfin[0].astype(F32)
    otk[...] = tfin[1].astype(F32)
    otv[...] = tfin[2].astype(F32)

    for i in range(1, 16):
        piece = fin.at[around(i, -1)]
        pltpu.make_async_copy(piece, piece, p4_r.at[i]).wait()
    for h in range(16):
        cols = slice(h * HD, (h + 1) * HD)
        oq[:, cols] = fin[h, 0].astype(F32)
        ok[:, cols] = fin[h, 1].astype(F32)
        ov[:, cols] = fin[h, 2].astype(F32)
    for c in sends:
        c.wait_send()


def per_device(*args):
    anyspace = pl.BlockSpec(memory_space=pl.ANY)
    vmem = pl.BlockSpec(memory_space=pltpu.VMEM)
    sem = pltpu.SemaphoreType.DMA
    V = pltpu.VMEM
    return pl.pallas_call(
        body,
        out_shape=[jax.ShapeDtypeStruct((16, 2048), F32)] * 3 + [jax.ShapeDtypeStruct((32, HD), F32)] * 3,
        in_specs=[anyspace] * 8,
        out_specs=[vmem] * 6,
        scratch_shapes=[
            V((4, 16, 2048), BF), V((16, 4, 16, HD), BF), V((16, 4, 16, HD), BF),
            V((3, 16, 2, 16, HD), BF), V((3, 16, 2, 16, HD), BF), V((4, 128, HD), BF),
            V((ROWS, HD), BF), V((ROWS, HD), BF), V((ROWS, HD), BF), V((ROWS, HD), BF), V((HD, ROWS), BF),
            V((ROWS, ROWS), F32), V((ROWS, ROWS), F32), V((ROWS, ROWS), BF), V((ROWS, ROWS), BF),
            V((8, ROWS), F32), V((8, ROWS), F32), V((8, ROWS), F32), V((32, HD), F32), V((3, 32, HD), F32),
            V((3, 2, 256, HD), BF), V((3, 2, 256, HD), BF), V((3, 2, 32, HD), BF), V((3, 2, 32, HD), BF),
            V((2, 256, HD), F32), V((2, 32, HD), F32),
            V((3, HD, 256), BF), V((3, HD, 256), BF), V((3, 32, HD), BF), V((3, 32, HD), BF),
            V((HD, 256), F32), V((32, HD), F32), V((HD, HD), F32),
            V((16, 3, 16, HD), BF), V((16, 3, 16, HD), BF), V((3, 32, HD), BF), V((3, 32, HD), BF),
            sem((4,)), sem((4, 4)),
            sem((16,)), sem((16,)), sem((4, 3)), sem((4, 3)), sem((4, 3)), sem((4, 3)), sem((3,)), sem((3,)),
            sem((3,)), sem((3,)), sem((3,)), sem((3,)), sem((3,)), sem((3,)), sem((3,)), sem((3,)),
            sem((16,)), sem((16,)), sem, sem,
        ],
        compiler_params=pltpu.CompilerParams(
            collective_id=0, has_side_effects=True, vmem_limit_bytes=50 * 1024 * 1024),
        cost_estimate=pl.CostEstimate(flops=1_700_000_000, bytes_accessed=2_000_000, transcendentals=1_300_000),
    )(*args)


def solution(mesh):
    tokens = P(("seq", "mlp"), None)
    return jax.shard_map(
        per_device,
        mesh=mesh,
        in_specs=(P(), P(), P(), P(), tokens, tokens, tokens, tokens),
        out_specs=(tokens, tokens, tokens, P("mlp", "seq"), P("mlp", "seq"), P("mlp", "seq")),
        check_vma=False,
    )
```

```python
import jax
import jax.numpy as jnp
from jax import lax
from jax.experimental import pallas as pl
from jax.experimental.pallas import tpu as pltpu
from jax.sharding import PartitionSpec as P

HD = 128
LOG2E = 1.4426950408889634
SCALE = HD ** -0.5
UNIT = SCALE * LOG2E
BF = jnp.bfloat16
F32 = jnp.float32
MESH = pl.DeviceIdType.MESH

START = (0, 128, 384, 640, 896)
SIZE = (128, 256, 256, 256, 256)
ROWS = 1152


def nt(a, b):
    return lax.dot_general(a, b, (((1,), (1,)), ((), ())), preferred_element_type=F32)


def nn(a, b):
    return lax.dot_general(a, b, (((1,), (0,)), ((), ())), preferred_element_type=F32)


def body(
    tq, tk, tv, tg, iq, ik, iv, ig,
    fin, tfin,
    flat, stage, own, qg, kv, text,
    qall, kall, vall, gall, ktall,
    e_buf, dp_buf, pb_buf, ds_buf, mx, sm, dl, st, st_in,
    dkv_st, dkv_in, dkv_own, dkvt_st, dkvt_in, dkvt_own,
    dq_st, dq_in, dq_own, dqt_st, dqt_in, dq_text,
    out_st, tout,
    in_sem, text_sem,
    p1_s, p1_r, near_r, qg_s, qg_r, kv_s, kv_r, st_s, st_r,
    dkv_s, dkv_r, dkvt_s, dkvt_r, dq_s, dq_r, dqt_s, dqt_r,
    p4_s, p4_r, tx_s, tx_r,
):
    s = lax.axis_index("seq")
    m = lax.axis_index("mlp")
    z0, y, core = s // 8, (s // 2) % 4, s % 2
    x, zh = m // 4, m % 4

    def flip(j):
        zf = 1 - z0 if j & 2 else z0
        cf = 1 - core if j & 1 else core
        return zf * 8 + y * 2 + cf

    def turn(j):
        return z0 * 8 + ((y + j) % 4) * 2 + core

    def around(i, sign):
        dz, dx = i // 4, i % 4
        return ((x + sign * dx + 4) % 4) * 4 + (zh + sign * dz + 4) % 4

    far_first = (10, 9, 11, 8, 6, 14, 5, 13, 7, 15, 4, 12, 2, 1, 3)
    sends = []

    def send(src, dst, ss, rs, seq, mlp):
        c = pltpu.make_async_remote_copy(
            src, dst, ss, rs, device_id={"seq": seq, "mlp": mlp}, device_id_type=MESH)
        c.start()
        sends.append(c)

    def arrive(ref, sem):
        pltpu.make_async_copy(ref, ref, sem).wait()

    loads = []
    for n, ref in enumerate((iq, ig, ik, iv)):
        c = pltpu.make_async_copy(ref, flat.at[n], in_sem.at[n])
        c.start()
        loads.append(c)

    barrier = pltpu.get_barrier_semaphore()
    for i in far_first:
        pl.semaphore_signal(barrier, inc=1, device_id={"seq": s, "mlp": around(i, 1)}, device_id_type=MESH)

    @pl.when(s != m)
    def _():
        pl.semaphore_signal(barrier, inc=1, device_id={"seq": m, "mlp": s}, device_id_type=MESH)

    for j in (2, 3, 1):
        pl.semaphore_signal(barrier, inc=1, device_id={"seq": turn(j), "mlp": m}, device_id_type=MESH)
        pl.semaphore_signal(barrier, inc=1, device_id={"seq": flip(j), "mlp": m}, device_id_type=MESH)

    for n, c in enumerate(loads):
        c.wait()
        for h in range(16):
            stage[h, n] = flat[n, :, h * HD:(h + 1) * HD]

    @pl.when(s != m)
    def _():
        pl.semaphore_wait(barrier, 22)

    @pl.when(s == m)
    def _():
        pl.semaphore_wait(barrier, 21)

    for i in (1, 3, 2, 10, 9, 11, 8, 6, 14, 5, 13, 7, 15, 4, 12):
        dest = around(i, -1)
        send(stage.at[dest], own.at[i], p1_s.at[i], p1_r.at[i], s, dest)
    own[0] = stage[m]

    col = pl.ds(pl.multiple_of(m * HD, HD), HD)
    tloads = []
    for n, ref in enumerate((tq, tg, tk, tv)):
        for j in range(4):
            owner = (j // 2) * 8 + y * 2 + j % 2 if n < 2 else turn((4 - j) % 4)
            rows = pl.ds(pl.multiple_of(owner * 32, 32), 32)
            c = pltpu.make_async_copy(ref.at[rows, col], text.at[n, pl.ds(j * 32, 32)], text_sem.at[n, j])
            c.start()
            tloads.append(c)
    for c in tloads:
        c.wait()
    qall[0:128] = text[0]
    gall[0:128] = text[1]
    kall[0:128] = text[2]
    vall[0:128] = text[3]

    def copy(src, dst, ss, rs, seq):
        pltpu.make_async_remote_copy(
            src, dst, ss, rs, device_id={"seq": seq, "mlp": m}, device_id_type=MESH).start()

    def relay(g):
        part = pl.ds(4 * g, 4)
        arrive(qg.at[1, part], near_r.at[g])
        copy(qg.at[1, part], qg.at[2, part], qg_s.at[2], qg_r.at[2], flip(1))

    for n, i in enumerate((0, 1, 3, 2, 4, 12, 5, 13, 7, 15, 6, 14, 8, 9, 11, 10)):
        if i:
            arrive(own.at[i], p1_r.at[i])
        for j in (2, 1, 3):
            copy(own.at[i, pl.ds(2, 2)], kv.at[j - 1, i], kv_s.at[j - 1], kv_r.at[j - 1], turn(j))
        copy(own.at[i, pl.ds(0, 2)], qg.at[1, i], qg_s.at[1], near_r.at[i // 4], flip(2))
        copy(own.at[i, pl.ds(0, 2)], qg.at[0, i], qg_s.at[0], qg_r.at[0], flip(1))
        if n == 12:
            relay(0)

    def query_rows(qc):
        return pl.ds(START[qc], SIZE[qc])

    def width(qc):
        return 128 if qc == 0 else 256

    def key_rows(kc):
        return pl.ds(START[kc], SIZE[kc])

    def pass_one(kc, qc):
        kr, qr, n = key_rows(kc), query_rows(qc), pl.ds(0, width(qc))
        scores = nt(kall[kr], qall[qr])
        top = jnp.max(scores, axis=0, keepdims=True)
        e = jnp.exp2((scores - top) * UNIT)
        dp = nt(vall[kr], gall[qr])
        mx[qc, kc:kc + 1, n] = top
        sm[qc, kc:kc + 1, n] = jnp.sum(e, axis=0, keepdims=True)
        dl[qc, kc:kc + 1, n] = jnp.sum(e * dp, axis=0, keepdims=True)
        e_buf[qc, kr, n] = e
        dp_buf[qc, kr, n] = dp

    def take_keys(j):
        if j:
            arrive(kv.at[j - 1], kv_r.at[j - 1])
            k, v = kv[j - 1, :, 0], kv[j - 1, :, 1]
        else:
            k, v = own[:, 2], own[:, 3]
        r = key_rows(j + 1)
        kall[r] = k.reshape(256, HD)
        vall[r] = v.reshape(256, HD)

    def take_queries(j):
        if j:
            if j != 2:
                arrive(qg.at[j - 1], qg_r.at[j - 1])
            q, g_ = qg[j - 1, :, 0], qg[j - 1, :, 1]
        else:
            q, g_ = own[:, 0], own[:, 1]
        r = query_rows(j + 1)
        qall[r] = q.reshape(256, HD)
        gall[r] = g_.reshape(256, HD)

    take_queries(0)
    take_keys(0)
    for kc in (0, 1):
        pass_one(kc, 0)
        pass_one(kc, 1)
    take_queries(1)
    for kc in (0, 1):
        pass_one(kc, 2)
    relay(1)
    relay(3)
    relay(2)
    take_queries(2)
    for kc in (0, 1):
        pass_one(kc, 3)
    for j in (1, 3):
        take_keys(j)
        pass_one(j + 1, 0)
        for i in range(3):
            pass_one(j + 1, i + 1)
    take_queries(3)
    for kc in (0, 1, 2, 4):
        pass_one(kc, 4)
    take_keys(2)

    for qc in range(5):
        pass_one(3, qc)
        n = pl.ds(0, width(qc))
        top = jnp.max(mx[qc, 0:5, n], axis=0, keepdims=True)
        w = jnp.exp2((mx[qc, 0:5, n] - top) * UNIT)
        total = jnp.sum(w * sm[qc, 0:5, n], axis=0, keepdims=True)
        dsum = jnp.sum(w * dl[qc, 0:5, n], axis=0, keepdims=True)
        for i, row in enumerate((top, total, dsum)):
            for half in range(1 if qc == 0 else 2):
                b = 2 * qc - 1 + half if qc else 0
                st[i * 9 + b:i * 9 + b + 1] = row[:, half * 128:(half + 1) * 128]
    for j in (2, 3, 1):
        send(st, st_in.at[j - 1], st_s.at[j - 1], st_r.at[j - 1], flip(j), m)
    ktall[...] = kall[...].T
    for j in (1, 2, 3):
        arrive(st_in.at[j - 1], st_r.at[j - 1])

    def theirs(j, first):
        rows = [0] + [1 + 2 * (r ^ j) + half for r in range(4) for half in range(2)]
        return jnp.concatenate([st_in[j - 1, first + b:first + b + 1] for b in rows], axis=0)

    tops, sums, dsums = ([st[n:n + 9]] + [theirs(j, n) for j in (1, 2, 3)] for n in (0, 9, 18))
    gtop = jnp.maximum(jnp.maximum(tops[0], tops[1]), jnp.maximum(tops[2], tops[3]))
    ws = [jnp.exp2((t - gtop) * UNIT) for t in tops]
    gsum = sum(w * t for w, t in zip(ws, sums))
    gd = sum(w * t for w, t in zip(ws, dsums))
    inv = 1.0 / gsum

    delta = gd * inv

    def as_row(a, qc):
        if qc == 0:
            return a[0:1]
        return jnp.concatenate([a[2 * qc - 1:2 * qc], a[2 * qc:2 * qc + 1]], axis=1)

    for qc in range(5):
        n = pl.ds(0, width(qc))
        mx[qc, 0:5, n] = jnp.exp2((mx[qc, 0:5, n] - as_row(gtop, qc)) * UNIT) * as_row(inv, qc)
        dl[qc, 0:1, n] = as_row(delta, qc)

    def probs(kc, qc):
        kr, qr, n = key_rows(kc), query_rows(qc), pl.ds(0, width(qc))
        p = e_buf[qc, kr, n] * mx[qc, kc:kc + 1, n]
        pb_buf[kr, qr] = p.astype(BF)
        ds_buf[kr, qr] = (p * (dp_buf[qc, kr, n] - dl[qc, 0:1, n])).astype(BF)

    def value_grad(kc):
        return nn(pb_buf[key_rows(kc)], gall[...])

    def key_grad(kc):
        return nn(ds_buf[key_rows(kc)], qall[...]) * SCALE

    def query_grad(qc):
        return (nn(ktall[...], ds_buf[:, query_rows(qc)]) * SCALE).T

    def text_part(j):
        peer = flip(j)
        return pl.ds(pl.multiple_of((peer // 8 * 2 + peer % 2) * 32, 32), 32)

    def group(g):
        return pl.ds(64 * g, 64)

    FAR = (2, 1, 3, 0)

    def keys_out(kc):
        j = kc - 1
        dv, dk = value_grad(kc).astype(BF), key_grad(kc).astype(BF)
        for g in FAR:
            dkv_st[j - 1, g, 0] = dk[64 * g:64 * g + 64]
            dkv_st[j - 1, g, 1] = dv[64 * g:64 * g + 64]
            send(dkv_st.at[j - 1, g], dkv_in.at[j - 1, g], dkv_s.at[j - 1, g], dkv_r.at[j - 1, g], turn(4 - j), m)

    for qc in range(5):
        probs(0, qc)
    dk, dv = key_grad(0), value_grad(0)
    dkvt_own[0] = dk[0:32]
    dkvt_own[1] = dv[0:32]
    for j in (2, 1, 3):
        part = slice(j * 32, j * 32 + 32)
        dkvt_st[j - 1, 0] = dk[part].astype(BF)
        dkvt_st[j - 1, 1] = dv[part].astype(BF)
        send(dkvt_st.at[j - 1], dkvt_in.at[j - 1], dkvt_s.at[j - 1], dkvt_r.at[j - 1], turn(4 - j), m)
    for qc in range(5):
        probs(3, qc)
    keys_out(3)
    for kc in (2, 4, 1):
        probs(kc, 0)
    dq_text[...] = query_grad(0)
    for j in (2, 3, 1):
        dqt_st[j - 1] = dq_text[text_part(j)].astype(BF)
        send(dqt_st.at[j - 1], dqt_in.at[j - 1], dqt_s.at[j - 1], dqt_r.at[j - 1], flip(j), m)
    for kc in (2, 4):
        for qc in range(1, 5):
            probs(kc, qc)
        keys_out(kc)
    for qc in range(1, 5):
        probs(1, qc)

    for j in (2, 3, 1, 0):
        dq = query_grad(j + 1)
        if j == 0:
            dq_own[...] = dq
            continue
        dq_st[j - 1] = dq.astype(BF)
        for g in FAR:
            rows = group(g)
            send(dq_st.at[j - 1, rows], dq_in.at[j - 1, rows], dq_s.at[j - 1, g], dq_r.at[j - 1, g], flip(j), m)

    own_v = value_grad(1)
    own_k = key_grad(1)
    dkv_own[0] = own_k
    dkv_own[1] = own_v

    for j in range(3):
        arrive(dqt_in.at[j], dqt_r.at[j])
        arrive(dkvt_in.at[j], dkvt_r.at[j])

    def plus(own_term, terms):
        for t in terms:
            own_term = own_term + t.astype(F32)
        return own_term

    tout[0] = plus(dq_text[text_part(0)], [dqt_in[j] for j in range(3)]).astype(BF)
    tout[1] = plus(dkvt_own[0], [dkvt_in[j, 0] for j in range(3)]).astype(BF)
    tout[2] = plus(dkvt_own[1], [dkvt_in[j, 1] for j in range(3)]).astype(BF)
    tcopy = pltpu.make_async_remote_copy(
        tout, tfin, tx_s, tx_r, device_id={"seq": m, "mlp": s}, device_id_type=MESH)

    @pl.when(s != m)
    def _():
        tcopy.start()

    @pl.when(s == m)
    def _():
        tfin[...] = tout[...]

    for g in FAR:
        slots = pl.ds(4 * g, 4)
        for j in range(3):
            arrive(dkv_in.at[j, g], dkv_r.at[j, g])
        for n in (0, 1):
            total = plus(dkv_own[n, group(g)], [dkv_in[j, g, n] for j in range(3)])
            out_st[slots, n + 1] = total.astype(BF).reshape(4, 16, HD)
        for j in range(3):
            arrive(dq_in.at[j, group(g)], dq_r.at[j, g])
        total = plus(dq_own[group(g)], [dq_in[j, group(g)] for j in range(3)])
        out_st[slots, 0] = total.astype(BF).reshape(4, 16, HD)
        for i in (4 * g + 2, 4 * g + 1, 4 * g + 3, 4 * g):
            if i:
                send(out_st.at[i], fin.at[m], p4_s.at[i], p4_r.at[i], s, around(i, 1))
    fin[m] = out_st[0]

    for j in range(3):
        arrive(kv.at[j], kv_s.at[j])
        arrive(qg.at[j], qg_s.at[j])
    for c in sends:
        c.wait_send()
    for i in far_first:
        arrive(fin.at[around(i, -1)], p4_r.at[i])

    @pl.when(s != m)
    def _():
        tcopy.wait()


def widen(fin, tfin, oq, ok, ov, otq, otk, otv):
    for n, out in enumerate((oq, ok, ov)):
        for h in range(16):
            out[:, h * HD:(h + 1) * HD] = fin[h, n].astype(F32)
    for n, out in enumerate((otq, otk, otv)):
        out[...] = tfin[n].astype(F32)


def per_device(*args):
    hbm = pl.BlockSpec(memory_space=pltpu.HBM)
    vmem = pl.BlockSpec(memory_space=pltpu.VMEM)
    sem = pltpu.SemaphoreType.DMA
    V = pltpu.VMEM
    landed = pl.pallas_call(
        body,
        out_shape=[pltpu.VMEM((16, 3, 16, HD), BF), pltpu.VMEM((3, 32, HD), BF)],
        in_specs=[hbm] * 8,
        out_specs=[vmem] * 2,
        scratch_shapes=[
            V((4, 16, 2048), BF), V((16, 4, 16, HD), BF), V((16, 4, 16, HD), BF),
            V((3, 16, 2, 16, HD), BF), V((3, 16, 2, 16, HD), BF), V((4, 128, HD), BF),
            V((ROWS, HD), BF), V((ROWS, HD), BF), V((ROWS, HD), BF), V((ROWS, HD), BF), V((HD, ROWS), BF),
            V((5, ROWS, 256), F32), V((5, ROWS, 256), F32), V((ROWS, ROWS), BF), V((ROWS, ROWS), BF),
            V((5, 8, 256), F32), V((5, 8, 256), F32), V((5, 8, 256), F32), V((32, HD), F32), V((3, 32, HD), F32),
            V((3, 4, 2, 64, HD), BF), V((3, 4, 2, 64, HD), BF), V((2, 256, HD), F32),
            V((3, 2, 32, HD), BF), V((3, 2, 32, HD), BF), V((2, 32, HD), F32),
            V((3, 256, HD), BF), V((3, 256, HD), BF), V((256, HD), F32),
            V((3, 32, HD), BF), V((3, 32, HD), BF), V((HD, HD), F32),
            V((16, 3, 16, HD), BF), V((3, 32, HD), BF),
            sem((4,)), sem((4, 4)),
            sem((16,)), sem((16,)), sem((4,)), sem((3,)), sem((3,)), sem((3,)), sem((3,)), sem((3,)), sem((3,)),
            sem((3, 4)), sem((3, 4)), sem((3,)), sem((3,)), sem((3, 4)), sem((3, 4)), sem((3,)), sem((3,)),
            sem((16,)), sem((16,)), sem, sem,
        ],
        compiler_params=pltpu.CompilerParams(
            collective_id=0, has_side_effects=True, vmem_limit_bytes=48 * 1024 * 1024),
        cost_estimate=pl.CostEstimate(flops=1_700_000_000, bytes_accessed=2_000_000, transcendentals=1_300_000),
    )(*[pltpu.with_memory_space_constraint(a, pltpu.HBM) for a in args])
    return pl.pallas_call(
        widen,
        out_shape=[jax.ShapeDtypeStruct((16, 2048), F32)] * 3 + [jax.ShapeDtypeStruct((32, HD), F32)] * 3,
        in_specs=[vmem] * 2,
        out_specs=[vmem] * 6,
        compiler_params=pltpu.CompilerParams(vmem_limit_bytes=4 * 1024 * 1024),
    )(*landed)


def solution(mesh):
    tokens = P(("seq", "mlp"), None)
    return jax.shard_map(
        per_device,
        mesh=mesh,
        in_specs=(P(), P(), P(), P(), tokens, tokens, tokens, tokens),
        out_specs=(tokens, tokens, tokens, P("mlp", "seq"), P("mlp", "seq"), P("mlp", "seq")),
        check_vma=False,
    )
```

```python
import jax
import jax.numpy as jnp
from jax import lax
from jax.experimental import pallas as pl
from jax.experimental.pallas import tpu as pltpu
from jax.sharding import PartitionSpec as P

HD = 128
LOG2E = 1.4426950408889634
SCALE = HD ** -0.5
UNIT = SCALE * LOG2E
BF = jnp.bfloat16
F32 = jnp.float32
MESH = pl.DeviceIdType.MESH

SLOTS = ((0, 0), (0, 1), (1, 0), (7, 0), (1, 1), (7, 1), (2, 0), (6, 0),
         (2, 1), (6, 1), (3, 0), (5, 0), (3, 1), (5, 1), (4, 0), (4, 1))

START = (0, 128, 384, 640, 896)
SIZE = (128, 256, 256, 256, 256)
ROWS = 1152


def nt(a, b):
    return lax.dot_general(a, b, (((1,), (1,)), ((), ())), preferred_element_type=F32)


def nn(a, b):
    return lax.dot_general(a, b, (((1,), (0,)), ((), ())), preferred_element_type=F32)


def body(
    tq, tk, tv, tg, iq, ik, iv, ig,
    fin, tfin,
    flat, stage, own, qg, kv, text,
    qall, kall, vall, gall, ktall,
    e_buf, dp_buf, pb_buf, ds_buf, mx, sm, dl, st, st_in,
    dkv_st, dkv_in, dkv_own, dkvt_st, dkvt_in, dkvt_own,
    dq_st, dq_in, dq_own, dqt_st, dqt_in, dq_text,
    out_st, tout,
    in_sem, text_sem,
    p1_s, p1_r, qg_s, qg_r, ql, kv_s, kv_r, st_s, st_r,
    dkv_s, dkv_r, dkvt_s, dkvt_r, dq_s, dq_r, dqt_s, dqt_r,
    p4_s, p4_r, tx_s, tx_r,
):
    seq = lax.axis_index("seq")
    mlp = lax.axis_index("mlp")
    z0, y, core = seq // 8, (seq // 2) % 4, seq % 2
    x, zh = mlp // 4, mlp % 4
    z = zh * 2 + z0

    head = z0 * 8 + zh * 2 + core
    u = x * (1 - core) + y * core
    v = y * (1 - core) + x * core

    def along(jx, jy):
        return {"seq": z0 * 8 + ((y + jy) % 4) * 2 + core, "mlp": ((x + jx) % 4) * 4 + zh}

    def shift(j):
        return along(j * (1 - core), j * core)

    def turn(j):
        return along(j * core, j * (1 - core))

    def block(a, b):
        return a * (4 - 3 * core) + b * (1 + 3 * core)

    def around(i, sign):
        dz, dc = SLOTS[i]
        there = (z + sign * dz + 8) % 8
        other = 1 - core if dc else core
        return there % 2, there // 2, other

    def column(i, sign):
        zo, zi, other = around(i, sign)
        return {"seq": zo * 8 + y * 2 + other, "mlp": x * 4 + zi}

    def head_of(i, sign):
        zo, zi, other = around(i, sign)
        return zo * 8 + zi * 2 + other

    partner = {"seq": z0 * 8 + zh * 2 + core, "mlp": x * 4 + y}
    sends = []

    def send(src, dst, ss, rs, to):
        c = pltpu.make_async_remote_copy(src, dst, ss, rs, device_id=to, device_id_type=MESH)
        c.start()
        sends.append(c)

    def arrive(ref, sem):
        pltpu.make_async_copy(ref, ref, sem).wait()

    loads = []
    for n, ref in enumerate((iq, ig, ik, iv)):
        c = pltpu.make_async_copy(ref, flat.at[n], in_sem.at[n])
        c.start()
        loads.append(c)

    barrier = pltpu.get_barrier_semaphore()
    def greet(to):
        pl.semaphore_signal(barrier, inc=1, device_id=to, device_id_type=MESH)

    for i in range(15, 0, -1):
        greet(column(i, 1))

    @pl.when(y != zh)
    def _():
        greet(partner)

    for j in (2, 3, 1):
        greet(turn(j))
        greet(shift(j))

    for n, c in enumerate(loads):
        c.wait()
        for h in range(16):
            stage[h, n] = flat[n, :, h * HD:(h + 1) * HD]

    @pl.when(y != zh)
    def _():
        pl.semaphore_wait(barrier, 22)

    @pl.when(y == zh)
    def _():
        pl.semaphore_wait(barrier, 21)

    for i in range(1, 16):
        send(stage.at[head_of(i, -1)], own.at[i], p1_s.at[i], p1_r.at[i], column(i, -1))
    own[0] = stage[head]

    col = pl.ds(pl.multiple_of(head * HD, HD), HD)
    tloads = []
    for n, ref in enumerate((tq, tg, tk, tv)):
        for j in range(4):
            owner = block(j, v) if n < 2 else block(u, (v + 4 - j) % 4)
            rows = pl.ds(pl.multiple_of(owner * 32, 32), 32)
            c = pltpu.make_async_copy(ref.at[rows, col], text.at[n, pl.ds(j * 32, 32)], text_sem.at[n, j])
            c.start()
            tloads.append(c)
    for c in tloads:
        c.wait()
    qall[0:128] = text[0]
    gall[0:128] = text[1]
    kall[0:128] = text[2]
    vall[0:128] = text[3]

    for i in range(16):
        if i:
            arrive(own.at[i], p1_r.at[i])
        g = i // 4
        for j in (2, 1, 3):
            pltpu.make_async_remote_copy(
                own.at[i, pl.ds(2, 2)], kv.at[j - 1, i], kv_s.at[j - 1], kv_r.at[j - 1, g],
                device_id=turn(j), device_id_type=MESH).start()
            pltpu.make_async_remote_copy(
                own.at[i, pl.ds(0, 2)], qg.at[u, i], qg_s.at[j - 1], qg_r.at[u, g],
                device_id=shift(j), device_id_type=MESH).start()
        pltpu.make_async_copy(own.at[i, pl.ds(0, 2)], qg.at[u, i], ql.at[g]).start()

    def query_rows(qc):
        return pl.ds(START[qc], SIZE[qc])

    def width(qc):
        return 128 if qc == 0 else 256

    def key_rows(kc):
        return pl.ds(START[kc], SIZE[kc])

    def pass_one(kc, qc):
        kr, qr, n = key_rows(kc), query_rows(qc), pl.ds(0, width(qc))
        scores = nt(kall[kr], qall[qr])
        top = jnp.max(scores, axis=0, keepdims=True)
        e = jnp.exp2((scores - top) * UNIT)
        dp = nt(vall[kr], gall[qr])
        mx[qc, kc:kc + 1, n] = top
        sm[qc, kc:kc + 1, n] = jnp.sum(e, axis=0, keepdims=True)
        dl[qc, kc:kc + 1, n] = jnp.sum(e * dp, axis=0, keepdims=True)
        e_buf[qc, kr, n] = e
        dp_buf[qc, kr, n] = dp

    def take(g):
        slots = pl.ds(4 * g, 4)
        for j in range(1, 4):
            arrive(kv.at[j - 1, slots], kv_r.at[j - 1, g])
            a = (u + 4 - j) % 4
            arrive(qg.at[a, slots], qg_r.at[a, g])
        arrive(qg.at[u, slots], ql.at[g])
        for b in range(4):
            r = pl.ds(START[g + 1] + 64 * b, 64)
            k, val = (kv[b - 1, slots, 0], kv[b - 1, slots, 1]) if b else (own[slots, 2], own[slots, 3])
            kall[r] = k.reshape(64, HD)
            vall[r] = val.reshape(64, HD)
            qall[r] = qg[b, slots, 0].reshape(64, HD)
            gall[r] = qg[b, slots, 1].reshape(64, HD)

    pass_one(0, 0)
    for g in range(4):
        take(g)
        for c in range(g + 1):
            pass_one(g + 1, c)
            pass_one(c, g + 1)
        if g < 3:
            pass_one(g + 1, g + 1)

    for qc in range(5):
        if qc == 4:
            pass_one(4, 4)
        n = pl.ds(0, width(qc))
        top = jnp.max(mx[qc, 0:5, n], axis=0, keepdims=True)
        w = jnp.exp2((mx[qc, 0:5, n] - top) * UNIT)
        total = jnp.sum(w * sm[qc, 0:5, n], axis=0, keepdims=True)
        dsum = jnp.sum(w * dl[qc, 0:5, n], axis=0, keepdims=True)
        for i, row in enumerate((top, total, dsum)):
            for half in range(1 if qc == 0 else 2):
                b = 2 * qc - 1 + half if qc else 0
                st[i * 9 + b:i * 9 + b + 1] = row[:, half * 128:(half + 1) * 128]
    for j in (2, 3, 1):
        send(st, st_in.at[j - 1], st_s.at[j - 1], st_r.at[j - 1], shift(j))
    ktall[...] = kall[...].T
    for j in (1, 2, 3):
        arrive(st_in.at[j - 1], st_r.at[j - 1])

    tops, sums, dsums = ([st[n:n + 9]] + [st_in[j, n:n + 9] for j in range(3)] for n in (0, 9, 18))
    gtop = jnp.maximum(jnp.maximum(tops[0], tops[1]), jnp.maximum(tops[2], tops[3]))
    ws = [jnp.exp2((t - gtop) * UNIT) for t in tops]
    gsum = sum(w * t for w, t in zip(ws, sums))
    gd = sum(w * t for w, t in zip(ws, dsums))
    inv = 1.0 / gsum

    delta = gd * inv

    def as_row(a, qc):
        if qc == 0:
            return a[0:1]
        return jnp.concatenate([a[2 * qc - 1:2 * qc], a[2 * qc:2 * qc + 1]], axis=1)

    for qc in range(5):
        n = pl.ds(0, width(qc))
        mx[qc, 0:5, n] = jnp.exp2((mx[qc, 0:5, n] - as_row(gtop, qc)) * UNIT) * as_row(inv, qc)
        dl[qc, 0:1, n] = as_row(delta, qc)

    def probs(kc, qc):
        kr, qr, n = key_rows(kc), query_rows(qc), pl.ds(0, width(qc))
        p = e_buf[qc, kr, n] * mx[qc, kc:kc + 1, n]
        pb_buf[kr, qr] = p.astype(BF)
        ds_buf[kr, qr] = (p * (dp_buf[qc, kr, n] - dl[qc, 0:1, n])).astype(BF)

    def value_grad(kc):
        return nn(pb_buf[key_rows(kc)], gall[...])

    def key_grad(kc):
        return nn(ds_buf[key_rows(kc)], qall[...]) * SCALE

    def query_grad(qc):
        return (nn(ktall[...], ds_buf[:, query_rows(qc)]) * SCALE).T

    def text_part(j):
        return pl.ds(pl.multiple_of(((u + 4 - j) % 4) * 32, 32), 32)

    FAR = (3, 2, 1, 0)

    def keys_out(g):
        dk, dv = key_grad(g + 1), value_grad(g + 1)
        dkv_own[g, 0] = dk[0:64]
        dkv_own[g, 1] = dv[0:64]
        for j in (2, 1, 3):
            dkv_st[j - 1, g, 0] = dk[64 * j:64 * j + 64].astype(BF)
            dkv_st[j - 1, g, 1] = dv[64 * j:64 * j + 64].astype(BF)
            send(dkv_st.at[j - 1, g], dkv_in.at[j - 1, g], dkv_s.at[j - 1, g], dkv_r.at[j - 1, g], turn(4 - j))

    def queries_out(g):
        dq = query_grad(g + 1).reshape(4, 64, HD)
        dq_own[g] = dq
        dq_st[g] = dq.astype(BF)
        for j in (2, 1, 3):
            send(dq_st.at[g, (u + 4 - j) % 4], dq_in.at[j - 1, g], dq_s.at[j - 1, g], dq_r.at[j - 1, g], shift(4 - j))

    for g in (3, 2):
        for qc in range(5):
            probs(g + 1, qc)
        keys_out(g)
    for qc in range(5):
        probs(0, qc)
    dk, dv = key_grad(0), value_grad(0)
    dkvt_own[0] = dk[0:32]
    dkvt_own[1] = dv[0:32]
    for j in (2, 1, 3):
        part = slice(j * 32, j * 32 + 32)
        dkvt_st[j - 1, 0] = dk[part].astype(BF)
        dkvt_st[j - 1, 1] = dv[part].astype(BF)
        send(dkvt_st.at[j - 1], dkvt_in.at[j - 1], dkvt_s.at[j - 1], dkvt_r.at[j - 1], turn(4 - j))
    for kc in (2, 1):
        probs(kc, 0)
    dq_text[...] = query_grad(0)
    for j in (2, 1, 3):
        dqt_st[j - 1] = dq_text[text_part(j)].astype(BF)
        send(dqt_st.at[j - 1], dqt_in.at[j - 1], dqt_s.at[j - 1], dqt_r.at[j - 1], shift(4 - j))
    for g in (1, 0):
        for qc in range(1, 5):
            probs(g + 1, qc)
        keys_out(g)
    for g in FAR:
        queries_out(g)

    for j in range(3):
        arrive(dqt_in.at[j], dqt_r.at[j])
        arrive(dkvt_in.at[j], dkvt_r.at[j])

    def plus(own_term, terms):
        for t in terms:
            own_term = own_term + t.astype(F32)
        return own_term

    tout[0] = plus(dq_text[text_part(0)], [dqt_in[j] for j in range(3)]).astype(BF)
    tout[1] = plus(dkvt_own[0], [dkvt_in[j, 0] for j in range(3)]).astype(BF)
    tout[2] = plus(dkvt_own[1], [dkvt_in[j, 1] for j in range(3)]).astype(BF)
    tcopy = pltpu.make_async_remote_copy(
        tout, tfin, tx_s, tx_r, device_id=partner, device_id_type=MESH)

    @pl.when(y != zh)
    def _():
        tcopy.start()

    @pl.when(y == zh)
    def _():
        tfin[...] = tout[...]

    for g in FAR:
        slots = pl.ds(4 * g, 4)
        for j in range(3):
            arrive(dkv_in.at[j, g], dkv_r.at[j, g])
        for n in (0, 1):
            total = plus(dkv_own[g, n], [dkv_in[j, g, n] for j in range(3)])
            out_st[slots, n + 1] = total.astype(BF).reshape(4, 16, HD)
        for j in range(3):
            arrive(dq_in.at[j, g], dq_r.at[j, g])
        total = plus(dq_own[g, u], [dq_in[j, g] for j in range(3)])
        out_st[slots, 0] = total.astype(BF).reshape(4, 16, HD)
        for i in range(4 * g, 4 * g + 4):
            if i:
                send(out_st.at[i], fin.at[head], p4_s.at[i], p4_r.at[i], column(i, 1))
    fin[head] = out_st[0]

    for j in range(3):
        arrive(kv.at[j], kv_s.at[j])
        arrive(kv.at[j], qg_s.at[j])
    for c in sends:
        c.wait_send()
    for i in range(15, 0, -1):
        arrive(fin.at[head_of(i, -1)], p4_r.at[i])

    @pl.when(y != zh)
    def _():
        tcopy.wait()


def widen(fin, tfin, oq, ok, ov, otq, otk, otv):
    for n, out in enumerate((oq, ok, ov)):
        for h in range(16):
            out[:, h * HD:(h + 1) * HD] = fin[h, n].astype(F32)
    for n, out in enumerate((otq, otk, otv)):
        out[...] = tfin[n].astype(F32)


def per_device(*args):
    hbm = pl.BlockSpec(memory_space=pltpu.HBM)
    vmem = pl.BlockSpec(memory_space=pltpu.VMEM)
    sem = pltpu.SemaphoreType.DMA
    V = pltpu.VMEM
    landed = pl.pallas_call(
        body,
        out_shape=[pltpu.VMEM((16, 3, 16, HD), BF), pltpu.VMEM((3, 32, HD), BF)],
        in_specs=[hbm] * 8,
        out_specs=[vmem] * 2,
        scratch_shapes=[
            V((4, 16, 2048), BF), V((16, 4, 16, HD), BF), V((16, 4, 16, HD), BF),
            V((4, 16, 2, 16, HD), BF), V((3, 16, 2, 16, HD), BF), V((4, 128, HD), BF),
            V((ROWS, HD), BF), V((ROWS, HD), BF), V((ROWS, HD), BF), V((ROWS, HD), BF), V((HD, ROWS), BF),
            V((5, ROWS, 256), F32), V((5, ROWS, 256), F32), V((ROWS, ROWS), BF), V((ROWS, ROWS), BF),
            V((5, 8, 256), F32), V((5, 8, 256), F32), V((5, 8, 256), F32), V((32, HD), F32), V((3, 32, HD), F32),
            V((3, 4, 2, 64, HD), BF), V((3, 4, 2, 64, HD), BF), V((4, 2, 64, HD), F32),
            V((3, 2, 32, HD), BF), V((3, 2, 32, HD), BF), V((2, 32, HD), F32),
            V((4, 4, 64, HD), BF), V((3, 4, 64, HD), BF), V((4, 4, 64, HD), F32),
            V((3, 32, HD), BF), V((3, 32, HD), BF), V((HD, HD), F32),
            V((16, 3, 16, HD), BF), V((3, 32, HD), BF),
            sem((4,)), sem((4, 4)),
            sem((16,)), sem((16,)), sem((3,)), sem((4, 4)), sem((4,)), sem((3,)), sem((3, 4)), sem((3,)), sem((3,)),
            sem((3, 4)), sem((3, 4)), sem((3,)), sem((3,)), sem((3, 4)), sem((3, 4)), sem((3,)), sem((3,)),
            sem((16,)), sem((16,)), sem, sem,
        ],
        compiler_params=pltpu.CompilerParams(
            collective_id=0, has_side_effects=True, vmem_limit_bytes=48 * 1024 * 1024),
        cost_estimate=pl.CostEstimate(flops=1_700_000_000, bytes_accessed=2_000_000, transcendentals=1_300_000),
    )(*[pltpu.with_memory_space_constraint(a, pltpu.HBM) for a in args])
    return pl.pallas_call(
        widen,
        out_shape=[jax.ShapeDtypeStruct((16, 2048), F32)] * 3 + [jax.ShapeDtypeStruct((32, HD), F32)] * 3,
        in_specs=[vmem] * 2,
        out_specs=[vmem] * 6,
        compiler_params=pltpu.CompilerParams(vmem_limit_bytes=4 * 1024 * 1024),
    )(*landed)


def solution(mesh):
    tokens = P(("seq", "mlp"), None)
    return jax.shard_map(
        per_device,
        mesh=mesh,
        in_specs=(P(), P(), P(), P(), tokens, tokens, tokens, tokens),
        out_specs=(tokens, tokens, tokens, P("mlp", "seq"), P("mlp", "seq"), P("mlp", "seq")),
        check_vma=False,
    )
```

```python
import jax
import jax.numpy as jnp
from jax import lax
from jax.experimental import pallas as pl
from jax.experimental.pallas import tpu as pltpu
from jax.sharding import PartitionSpec as P

HD = 128
LOG2E = 1.4426950408889634
SCALE = HD ** -0.5
UNIT = SCALE * LOG2E
BF = jnp.bfloat16
F32 = jnp.float32
MESH = pl.DeviceIdType.MESH

SLOTS = ((0, 0), (0, 1), (1, 0), (7, 0), (1, 1), (7, 1), (2, 0), (6, 0),
         (2, 1), (6, 1), (3, 0), (5, 0), (3, 1), (5, 1), (4, 0), (4, 1))

START = (0, 128, 384, 640, 896)
SIZE = (128, 256, 256, 256, 256)
ROWS = 1152


def nt(a, b):
    return lax.dot_general(a, b, (((1,), (1,)), ((), ())), preferred_element_type=F32)


def nn(a, b):
    return lax.dot_general(a, b, (((1,), (0,)), ((), ())), preferred_element_type=F32)


def body(
    tq, tk, tv, tg, iq, ik, iv, ig,
    fin, tfin,
    flat, stage, own, qg, kv, text,
    qall, kall, vall, gall, ktall,
    e_buf, dp_buf, pb_buf, ds_buf, mx, sm, dl, st, st_in,
    dkv_st, dkv_in, dkv_own, dkvt_st, dkvt_in, dkvt_own,
    dq_st, dq_in, dq_own, dqt_st, dqt_in, dq_text,
    out_st, tout,
    in_sem, text_sem,
    p1_s, p1_r, qg_s, qg_r, kv_s, kv_r, st_s, st_r,
    dkv_s, dkv_r, dkvt_s, dkvt_r, dq_s, dq_r, dqt_s, dqt_r,
    p4_s, p4_r, tx_s, tx_r,
):
    seq = lax.axis_index("seq")
    mlp = lax.axis_index("mlp")
    z0, y, core = seq // 8, (seq // 2) % 4, seq % 2
    x, zh = mlp // 4, mlp % 4
    z = zh * 2 + z0

    head = z0 * 8 + zh * 2 + core
    u = x * (1 - core) + y * core
    v = y * (1 - core) + x * core

    def along(jx, jy):
        return {"seq": z0 * 8 + ((y + jy) % 4) * 2 + core, "mlp": ((x + jx) % 4) * 4 + zh}

    def shift(j):
        return along(j * (1 - core), j * core)

    def turn(j):
        return along(j * core, j * (1 - core))

    def block(a, b):
        return a * (4 - 3 * core) + b * (1 + 3 * core)

    def around(i, sign):
        dz, dc = SLOTS[i]
        there = (z + sign * dz + 8) % 8
        other = 1 - core if dc else core
        return there % 2, there // 2, other

    def column(i, sign):
        zo, zi, other = around(i, sign)
        return {"seq": zo * 8 + y * 2 + other, "mlp": x * 4 + zi}

    def head_of(i, sign):
        zo, zi, other = around(i, sign)
        return zo * 8 + zi * 2 + other

    partner = {"seq": z0 * 8 + zh * 2 + core, "mlp": x * 4 + y}
    sends = []

    def send(src, dst, ss, rs, to):
        c = pltpu.make_async_remote_copy(src, dst, ss, rs, device_id=to, device_id_type=MESH)
        c.start()
        sends.append(c)

    def arrive(ref, sem):
        pltpu.make_async_copy(ref, ref, sem).wait()

    loads = []
    for n, ref in enumerate((iq, ig, ik, iv)):
        c = pltpu.make_async_copy(ref, flat.at[n], in_sem.at[n])
        c.start()
        loads.append(c)

    col = pl.ds(pl.multiple_of(head * HD, HD), HD)
    tloads = []
    for n, ref in enumerate((tq, tg, tk, tv)):
        for j in range(4):
            owner = block(j, v) if n < 2 else block(u, (v + 4 - j) % 4)
            rows = pl.ds(pl.multiple_of(owner * 32, 32), 32)
            c = pltpu.make_async_copy(ref.at[rows, col], text.at[n, pl.ds(j * 32, 32)], text_sem.at[n, j])
            c.start()
            tloads.append(c)

    barrier = pltpu.get_barrier_semaphore()
    def greet(to):
        pl.semaphore_signal(barrier, inc=1, device_id=to, device_id_type=MESH)

    for i in range(15, 0, -1):
        greet(column(i, 1))

    for j in (2, 3, 1):
        greet(turn(j))
        greet(shift(j))

    for n, c in enumerate(loads):
        c.wait()
        for h in range(16):
            stage[h, n] = flat[n, :, h * HD:(h + 1) * HD]

    pl.semaphore_wait(barrier, 21)

    for i in range(1, 16):
        send(stage.at[head_of(i, -1)], own.at[i], p1_s.at[i], p1_r.at[i], column(i, -1))
    own[0] = stage[head]

    for i in range(16):
        if i:
            arrive(own.at[i], p1_r.at[i])
        g = i // 4
        for j in (2, 1, 3):
            pltpu.make_async_remote_copy(
                own.at[i, pl.ds(2, 2)], kv.at[j - 1, i], kv_s.at[j - 1], kv_r.at[j - 1, g],
                device_id=turn(j), device_id_type=MESH).start()
            pltpu.make_async_remote_copy(
                own.at[i, pl.ds(0, 2)], qg.at[u, i], qg_s.at[j - 1], qg_r.at[u, g],
                device_id=shift(j), device_id_type=MESH).start()

    def query_rows(qc):
        return pl.ds(START[qc], SIZE[qc])

    def width(qc):
        return 128 if qc == 0 else 256

    def key_rows(kc):
        return pl.ds(START[kc], SIZE[kc])

    def pass_one(kc, qc):
        kr, qr, n = key_rows(kc), query_rows(qc), pl.ds(0, width(qc))
        scores = nt(kall[kr], qall[qr])
        top = jnp.max(scores, axis=0, keepdims=True)
        e = jnp.exp2((scores - top) * UNIT)
        dp = nt(vall[kr], gall[qr])
        mx[qc, kc:kc + 1, n] = top
        sm[qc, kc:kc + 1, n] = jnp.sum(e, axis=0, keepdims=True)
        dl[qc, kc:kc + 1, n] = jnp.sum(e * dp, axis=0, keepdims=True)
        e_buf[qc, kr, n] = e
        dp_buf[qc, kr, n] = dp

    def take(g):
        slots = pl.ds(4 * g, 4)
        for j in range(1, 4):
            arrive(kv.at[j - 1, slots], kv_r.at[j - 1, g])
            a = (u + 4 - j) % 4
            arrive(qg.at[a, slots], qg_r.at[a, g])
        qg[u, slots] = own[slots, 0:2]
        for b in range(4):
            r = pl.ds(START[g + 1] + 64 * b, 64)
            k, val = (kv[b - 1, slots, 0], kv[b - 1, slots, 1]) if b else (own[slots, 2], own[slots, 3])
            kall[r] = k.reshape(64, HD)
            vall[r] = val.reshape(64, HD)
            qall[r] = qg[b, slots, 0].reshape(64, HD)
            gall[r] = qg[b, slots, 1].reshape(64, HD)

    for c in tloads:
        c.wait()
    qall[0:128] = text[0]
    gall[0:128] = text[1]
    kall[0:128] = text[2]
    vall[0:128] = text[3]
    pass_one(0, 0)
    for g in range(4):
        take(g)
        for c in range(g + 1):
            pass_one(g + 1, c)
            pass_one(c, g + 1)
        if g < 3:
            pass_one(g + 1, g + 1)

    for qc in range(5):
        if qc == 4:
            pass_one(4, 4)
        n = pl.ds(0, width(qc))
        top = jnp.max(mx[qc, 0:5, n], axis=0, keepdims=True)
        w = jnp.exp2((mx[qc, 0:5, n] - top) * UNIT)
        total = jnp.sum(w * sm[qc, 0:5, n], axis=0, keepdims=True)
        dsum = jnp.sum(w * dl[qc, 0:5, n], axis=0, keepdims=True)
        for i, row in enumerate((top, total, dsum)):
            for half in range(1 if qc == 0 else 2):
                b = 2 * qc - 1 + half if qc else 0
                st[i * 9 + b:i * 9 + b + 1] = row[:, half * 128:(half + 1) * 128]
    for j in (2, 3, 1):
        send(st, st_in.at[j - 1], st_s.at[j - 1], st_r.at[j - 1], shift(j))
    ktall[...] = kall[...].T
    for j in (1, 2, 3):
        arrive(st_in.at[j - 1], st_r.at[j - 1])

    tops, sums, dsums = ([st[n:n + 9]] + [st_in[j, n:n + 9] for j in range(3)] for n in (0, 9, 18))
    gtop = jnp.maximum(jnp.maximum(tops[0], tops[1]), jnp.maximum(tops[2], tops[3]))
    ws = [jnp.exp2((t - gtop) * UNIT) for t in tops]
    gsum = sum(w * t for w, t in zip(ws, sums))
    gd = sum(w * t for w, t in zip(ws, dsums))
    inv = 1.0 / gsum

    delta = gd * inv

    def as_row(a, qc):
        if qc == 0:
            return a[0:1]
        return jnp.concatenate([a[2 * qc - 1:2 * qc], a[2 * qc:2 * qc + 1]], axis=1)

    for qc in range(5):
        n = pl.ds(0, width(qc))
        mx[qc, 0:5, n] = jnp.exp2((mx[qc, 0:5, n] - as_row(gtop, qc)) * UNIT) * as_row(inv, qc)
        dl[qc, 0:1, n] = as_row(delta, qc)

    def probs(kc, qc):
        kr, qr, n = key_rows(kc), query_rows(qc), pl.ds(0, width(qc))
        p = e_buf[qc, kr, n] * mx[qc, kc:kc + 1, n]
        pb_buf[kr, qr] = p.astype(BF)
        ds_buf[kr, qr] = (p * (dp_buf[qc, kr, n] - dl[qc, 0:1, n])).astype(BF)

    def value_grad(kc):
        return nn(pb_buf[key_rows(kc)], gall[...])

    def key_grad(kc):
        return nn(ds_buf[key_rows(kc)], qall[...]) * SCALE

    def query_grad(qc):
        return (nn(ktall[...], ds_buf[:, query_rows(qc)]) * SCALE).T

    def text_part(j):
        return pl.ds(pl.multiple_of(((u + 4 - j) % 4) * 32, 32), 32)

    FAR = (3, 2, 1, 0)

    def keys_out(g):
        dk, dv = key_grad(g + 1), value_grad(g + 1)
        dkv_own[g, 0] = dk[0:64]
        dkv_own[g, 1] = dv[0:64]
        for j in (2, 1, 3):
            dkv_st[j - 1, g, 0] = dk[64 * j:64 * j + 64].astype(BF)
            dkv_st[j - 1, g, 1] = dv[64 * j:64 * j + 64].astype(BF)
            send(dkv_st.at[j - 1, g], dkv_in.at[j - 1, g], dkv_s.at[j - 1, g], dkv_r.at[j - 1, g], turn(4 - j))

    def queries_out(g):
        dq = query_grad(g + 1).reshape(4, 64, HD)
        dq_own[g] = dq
        dq_st[g] = dq.astype(BF)
        for j in (2, 1, 3):
            send(dq_st.at[g, (u + 4 - j) % 4], dq_in.at[j - 1, g], dq_s.at[j - 1, g], dq_r.at[j - 1, g], shift(4 - j))

    for g in FAR[:2]:
        for qc in range(5):
            probs(g + 1, qc)
        keys_out(g)
    for qc in range(5):
        probs(0, qc)
    dk, dv = key_grad(0), value_grad(0)
    dkvt_own[0] = dk[0:32]
    dkvt_own[1] = dv[0:32]
    for j in (2, 1, 3):
        part = slice(j * 32, j * 32 + 32)
        dkvt_st[j - 1, 0] = dk[part].astype(BF)
        dkvt_st[j - 1, 1] = dv[part].astype(BF)
        send(dkvt_st.at[j - 1], dkvt_in.at[j - 1], dkvt_s.at[j - 1], dkvt_r.at[j - 1], turn(4 - j))
    for g in FAR[2:]:
        probs(g + 1, 0)
    dq_text[...] = query_grad(0)
    for j in (2, 1, 3):
        dqt_st[j - 1] = dq_text[text_part(j)].astype(BF)
        send(dqt_st.at[j - 1], dqt_in.at[j - 1], dqt_s.at[j - 1], dqt_r.at[j - 1], shift(4 - j))
    for g in FAR[2:]:
        for qc in range(1, 5):
            probs(g + 1, qc)
        keys_out(g)
    for g in FAR:
        queries_out(g)

    def plus(own_term, terms):
        for t in terms:
            own_term = own_term + t.astype(F32)
        return own_term

    def hand_back(g, part):
        for i in range(4 * g, 4 * g + 4):
            if i:
                at, n, sems = (slice(0, 1), 1, 1) if part else (slice(1, 3), 2, 0)
                rows = pl.ds(at.start, n)
                send(out_st.at[i, rows], fin.at[head, rows], p4_s.at[sems, i], p4_r.at[sems, i], column(i, 1))

    def keys_back(g):
        slots = pl.ds(4 * g, 4)
        for j in range(3):
            arrive(dkv_in.at[j, g], dkv_r.at[j, g])
        for n in (0, 1):
            total = plus(dkv_own[g, n], [dkv_in[j, g, n] for j in range(3)])
            out_st[slots, n + 1] = total.astype(BF).reshape(4, 16, HD)
        hand_back(g, 0)

    def queries_back(g):
        slots = pl.ds(4 * g, 4)
        for j in range(3):
            arrive(dq_in.at[j, g], dq_r.at[j, g])
        total = plus(dq_own[g, u], [dq_in[j, g] for j in range(3)])
        out_st[slots, 0] = total.astype(BF).reshape(4, 16, HD)
        hand_back(g, 1)

    keys_back(FAR[0])
    keys_back(FAR[1])
    for j in range(3):
        arrive(dqt_in.at[j], dqt_r.at[j])
        arrive(dkvt_in.at[j], dkvt_r.at[j])

    tout[0] = plus(dq_text[text_part(0)], [dqt_in[j] for j in range(3)]).astype(BF)
    tout[1] = plus(dkvt_own[0], [dkvt_in[j, 0] for j in range(3)]).astype(BF)
    tout[2] = plus(dkvt_own[1], [dkvt_in[j, 1] for j in range(3)]).astype(BF)
    tcopy = pltpu.make_async_remote_copy(
        tout, tfin, tx_s, tx_r, device_id=partner, device_id_type=MESH)

    @pl.when(y != zh)
    def _():
        tcopy.start()

    @pl.when(y == zh)
    def _():
        tfin[...] = tout[...]

    keys_back(FAR[2])
    queries_back(FAR[0])
    keys_back(FAR[3])
    queries_back(FAR[1])
    queries_back(FAR[2])
    queries_back(FAR[3])
    fin[head] = out_st[0]

    for j in range(3):
        arrive(kv.at[j], kv_s.at[j])
        arrive(kv.at[j], qg_s.at[j])
    for c in sends:
        c.wait_send()
    for i in range(15, 0, -1):
        there = head_of(i, -1)
        arrive(fin.at[there, pl.ds(1, 2)], p4_r.at[0, i])
        arrive(fin.at[there, pl.ds(0, 1)], p4_r.at[1, i])

    @pl.when(y != zh)
    def _():
        tcopy.wait()


def widen(fin, tfin, oq, ok, ov, otq, otk, otv):
    for n, out in enumerate((oq, ok, ov)):
        for h in range(16):
            out[:, h * HD:(h + 1) * HD] = fin[h, n].astype(F32)
    for n, out in enumerate((otq, otk, otv)):
        out[...] = tfin[n].astype(F32)


def per_device(*args):
    hbm = pl.BlockSpec(memory_space=pltpu.HBM)
    vmem = pl.BlockSpec(memory_space=pltpu.VMEM)
    sem = pltpu.SemaphoreType.DMA
    V = pltpu.VMEM
    landed = pl.pallas_call(
        body,
        out_shape=[pltpu.VMEM((16, 3, 16, HD), BF), pltpu.VMEM((3, 32, HD), BF)],
        in_specs=[hbm] * 8,
        out_specs=[vmem] * 2,
        scratch_shapes=[
            V((4, 16, 2048), BF), V((16, 4, 16, HD), BF), V((16, 4, 16, HD), BF),
            V((4, 16, 2, 16, HD), BF), V((3, 16, 2, 16, HD), BF), V((4, 128, HD), BF),
            V((ROWS, HD), BF), V((ROWS, HD), BF), V((ROWS, HD), BF), V((ROWS, HD), BF), V((HD, ROWS), BF),
            V((5, ROWS, 256), F32), V((5, ROWS, 256), F32), V((ROWS, ROWS), BF), V((ROWS, ROWS), BF),
            V((5, 8, 256), F32), V((5, 8, 256), F32), V((5, 8, 256), F32), V((32, HD), F32), V((3, 32, HD), F32),
            V((3, 4, 2, 64, HD), BF), V((3, 4, 2, 64, HD), BF), V((4, 2, 64, HD), F32),
            V((3, 2, 32, HD), BF), V((3, 2, 32, HD), BF), V((2, 32, HD), F32),
            V((4, 4, 64, HD), BF), V((3, 4, 64, HD), BF), V((4, 4, 64, HD), F32),
            V((3, 32, HD), BF), V((3, 32, HD), BF), V((HD, HD), F32),
            V((16, 3, 16, HD), BF), V((3, 32, HD), BF),
            sem((4,)), sem((4, 4)),
            sem((16,)), sem((16,)), sem((3,)), sem((4, 4)), sem((3,)), sem((3, 4)), sem((3,)), sem((3,)),
            sem((3, 4)), sem((3, 4)), sem((3,)), sem((3,)), sem((3, 4)), sem((3, 4)), sem((3,)), sem((3,)),
            sem((2, 16)), sem((2, 16)), sem, sem,
        ],
        compiler_params=pltpu.CompilerParams(
            collective_id=0, has_side_effects=True, vmem_limit_bytes=48 * 1024 * 1024),
        cost_estimate=pl.CostEstimate(flops=1_700_000_000, bytes_accessed=2_000_000, transcendentals=1_300_000),
    )(*[pltpu.with_memory_space_constraint(a, pltpu.HBM) for a in args])
    return pl.pallas_call(
        widen,
        out_shape=[jax.ShapeDtypeStruct((16, 2048), F32)] * 3 + [jax.ShapeDtypeStruct((32, HD), F32)] * 3,
        in_specs=[vmem] * 2,
        out_specs=[vmem] * 6,
        compiler_params=pltpu.CompilerParams(vmem_limit_bytes=4 * 1024 * 1024),
    )(*landed)


def solution(mesh):
    tokens = P(("seq", "mlp"), None)
    return jax.shard_map(
        per_device,
        mesh=mesh,
        in_specs=(P(), P(), P(), P(), tokens, tokens, tokens, tokens),
        out_specs=(tokens, tokens, tokens, P("mlp", "seq"), P("mlp", "seq"), P("mlp", "seq")),
        check_vma=False,
    )
```

```python
import jax
import jax.numpy as jnp
from jax import lax
from jax.experimental import pallas as pl
from jax.experimental.pallas import tpu as pltpu
from jax.sharding import PartitionSpec as P

HD = 128
LOG2E = 1.4426950408889634
SCALE = HD ** -0.5
UNIT = SCALE * LOG2E
BF = jnp.bfloat16
F32 = jnp.float32
MESH = pl.DeviceIdType.MESH

SLOTS = ((0, 0), (0, 1), (1, 0), (7, 0), (1, 1), (7, 1), (2, 0), (6, 0),
         (2, 1), (6, 1), (3, 0), (5, 0), (3, 1), (5, 1), (4, 0), (4, 1))

START = (0, 128, 384, 640, 896)
SIZE = (128, 256, 256, 256, 256)
ROWS = 1152


def nt(a, b):
    return lax.dot_general(a, b, (((1,), (1,)), ((), ())), preferred_element_type=F32)


def nn(a, b):
    return lax.dot_general(a, b, (((1,), (0,)), ((), ())), preferred_element_type=F32)


def body(
    tq, tk, tv, tg, iq, ik, iv, ig,
    fin, tfin,
    flat, stage, own, qg, kv, text,
    qall, kall, vall, gall, ktall,
    e_buf, dp_buf, pb_buf, ds_buf, mx, sm, dl, st, st_in,
    dkv_st, dkv_in, dkv_own, dkvt_st, dkvt_in, dkvt_own,
    dq_st, dq_in, dq_own, dqt_st, dqt_in, dq_text,
    out_st, tout,
    in_sem, text_sem,
    p1_s, p1_r, qg_s, kv_s, p2_r, st_s, st_r,
    dkv_s, dkv_r, dkvt_s, dkvt_r, dq_s, dq_r, dqt_s, dqt_r,
    p4_s, p4_r, tx_s, tx_r,
):
    seq = lax.axis_index("seq")
    mlp = lax.axis_index("mlp")
    z0, y, core = seq // 8, (seq // 2) % 4, seq % 2
    x, zh = mlp // 4, mlp % 4
    z = zh * 2 + z0

    head = z0 * 8 + zh * 2 + core
    u = x * (1 - core) + y * core
    v = y * (1 - core) + x * core

    def along(jx, jy):
        return {"seq": z0 * 8 + ((y + jy) % 4) * 2 + core, "mlp": ((x + jx) % 4) * 4 + zh}

    def shift(j):
        return along(j * (1 - core), j * core)

    def turn(j):
        return along(j * core, j * (1 - core))

    def block(a, b):
        return a * (4 - 3 * core) + b * (1 + 3 * core)

    def around(i, sign):
        dz, dc = SLOTS[i]
        there = (z + sign * dz + 8) % 8
        other = 1 - core if dc else core
        return there % 2, there // 2, other

    def column(i, sign):
        zo, zi, other = around(i, sign)
        return {"seq": zo * 8 + y * 2 + other, "mlp": x * 4 + zi}

    def head_of(i, sign):
        zo, zi, other = around(i, sign)
        return zo * 8 + zi * 2 + other

    partner = {"seq": z0 * 8 + zh * 2 + core, "mlp": x * 4 + y}
    def send(src, dst, ss, rs, to):
        pltpu.make_async_remote_copy(src, dst, ss, rs, device_id=to, device_id_type=MESH).start()

    def arrive(ref, sem):
        pltpu.make_async_copy(ref, ref, sem).wait()

    for n, ref in enumerate((iq, ig, ik, iv)):
        pltpu.make_async_copy(ref, flat.at[n], in_sem).start()

    barrier = pltpu.get_barrier_semaphore()
    def greet(to):
        pl.semaphore_signal(barrier, inc=1, device_id=to, device_id_type=MESH)

    for i in range(15, 0, -1):
        greet(column(i, 1))

    for j in (2, 3, 1):
        greet(turn(j))
        greet(shift(j))

    col = pl.ds(pl.multiple_of(head * HD, HD), HD)
    for n, ref in enumerate((tq, tg, tk, tv)):
        for j in range(4):
            owner = block(j, v) if n < 2 else block(u, (v + 4 - j) % 4)
            rows = pl.ds(pl.multiple_of(owner * 32, 32), 32)
            pltpu.make_async_copy(ref.at[rows, col], text.at[n, pl.ds(j * 32, 32)], text_sem).start()

    arrive(flat, in_sem)
    for n in range(4):
        for h in range(16):
            stage[h, n] = flat[n, :, h * HD:(h + 1) * HD]

    pl.semaphore_wait(barrier, 21)

    for i in range(1, 16):
        send(stage.at[head_of(i, -1)], own.at[i], p1_s, p1_r.at[i - 1], column(i, -1))
    own[0] = stage[head]

    for i in range(16):
        if i:
            arrive(own.at[i], p1_r.at[i - 1])
        g = i // 4
        for j in (2, 1, 3):
            send(own.at[i, pl.ds(2, 2)], kv.at[j - 1, i], kv_s, p2_r.at[g], turn(j))
            send(own.at[i, pl.ds(0, 2)], qg.at[u, i], qg_s, p2_r.at[g], shift(j))

    def query_rows(qc):
        return pl.ds(START[qc], SIZE[qc])

    def width(qc):
        return 128 if qc == 0 else 256

    def key_rows(kc):
        return pl.ds(START[kc], SIZE[kc])

    def pass_one(kc, qc):
        kr, qr, n = key_rows(kc), query_rows(qc), pl.ds(0, width(qc))
        scores = nt(kall[kr], qall[qr])
        top = jnp.max(scores, axis=0, keepdims=True)
        e = jnp.exp2((scores - top) * UNIT)
        dp = nt(vall[kr], gall[qr])
        mx[qc, kc:kc + 1, n] = top
        sm[qc, kc:kc + 1, n] = jnp.sum(e, axis=0, keepdims=True)
        dl[qc, kc:kc + 1, n] = jnp.sum(e * dp, axis=0, keepdims=True)
        e_buf[qc, kr, n] = e
        dp_buf[qc, kr, n] = dp

    def take(g):
        slots = pl.ds(4 * g, 4)
        arrive(own.at[pl.ds(0, 12)], p2_r.at[g])
        qg[u, slots] = own[slots, 0:2]
        for b in range(4):
            r = pl.ds(START[g + 1] + 64 * b, 64)
            k, val = (kv[b - 1, slots, 0], kv[b - 1, slots, 1]) if b else (own[slots, 2], own[slots, 3])
            kall[r] = k.reshape(64, HD)
            vall[r] = val.reshape(64, HD)
            qall[r] = qg[b, slots, 0].reshape(64, HD)
            gall[r] = qg[b, slots, 1].reshape(64, HD)

    arrive(text, text_sem)
    qall[0:128] = text[0]
    gall[0:128] = text[1]
    kall[0:128] = text[2]
    vall[0:128] = text[3]
    pass_one(0, 0)
    for g in range(4):
        take(g)
        for c in range(g + 1):
            pass_one(g + 1, c)
            pass_one(c, g + 1)
        if g < 3:
            pass_one(g + 1, g + 1)

    for qc in range(5):
        if qc == 4:
            pass_one(4, 4)
        n = pl.ds(0, width(qc))
        top = jnp.max(mx[qc, 0:5, n], axis=0, keepdims=True)
        w = jnp.exp2((mx[qc, 0:5, n] - top) * UNIT)
        total = jnp.sum(w * sm[qc, 0:5, n], axis=0, keepdims=True)
        dsum = jnp.sum(w * dl[qc, 0:5, n], axis=0, keepdims=True)
        for i, row in enumerate((top, total, dsum)):
            for half in range(1 if qc == 0 else 2):
                b = 2 * qc - 1 + half if qc else 0
                st[i * 9 + b:i * 9 + b + 1] = row[:, half * 128:(half + 1) * 128]
    for j in (2, 3, 1):
        send(st, st_in.at[j - 1], st_s, st_r, shift(j))
    ktall[...] = kall[...].T
    arrive(st_in, st_r)

    tops, sums, dsums = ([st[n:n + 9]] + [st_in[j, n:n + 9] for j in range(3)] for n in (0, 9, 18))
    gtop = jnp.maximum(jnp.maximum(tops[0], tops[1]), jnp.maximum(tops[2], tops[3]))
    ws = [jnp.exp2((t - gtop) * UNIT) for t in tops]
    gsum = sum(w * t for w, t in zip(ws, sums))
    gd = sum(w * t for w, t in zip(ws, dsums))
    inv = 1.0 / gsum

    delta = gd * inv

    def as_row(a, qc):
        if qc == 0:
            return a[0:1]
        return jnp.concatenate([a[2 * qc - 1:2 * qc], a[2 * qc:2 * qc + 1]], axis=1)

    for qc in range(5):
        n = pl.ds(0, width(qc))
        mx[qc, 0:5, n] = jnp.exp2((mx[qc, 0:5, n] - as_row(gtop, qc)) * UNIT) * as_row(inv, qc)
        dl[qc, 0:1, n] = as_row(delta, qc)

    def probs(kc, qc):
        kr, qr, n = key_rows(kc), query_rows(qc), pl.ds(0, width(qc))
        p = e_buf[qc, kr, n] * mx[qc, kc:kc + 1, n]
        pb_buf[kr, qr] = p.astype(BF)
        ds_buf[kr, qr] = (p * (dp_buf[qc, kr, n] - dl[qc, 0:1, n])).astype(BF)

    def value_grad(kc):
        return nn(pb_buf[key_rows(kc)], gall[...])

    def key_grad(kc):
        return nn(ds_buf[key_rows(kc)], qall[...]) * SCALE

    def query_grad(qc):
        return (nn(ktall[...], ds_buf[:, query_rows(qc)]) * SCALE).T

    def text_part(j):
        return pl.ds(pl.multiple_of(((u + 4 - j) % 4) * 32, 32), 32)

    FAR = (3, 2, 1, 0)

    def keys_out(g):
        dk, dv = key_grad(g + 1), value_grad(g + 1)
        dkv_own[g, 0] = dk[0:64]
        dkv_own[g, 1] = dv[0:64]
        for j in (2, 1, 3):
            dkv_st[j - 1, g, 0] = dk[64 * j:64 * j + 64].astype(BF)
            dkv_st[j - 1, g, 1] = dv[64 * j:64 * j + 64].astype(BF)
            send(dkv_st.at[j - 1, g], dkv_in.at[j - 1, g], dkv_s, dkv_r.at[g], turn(4 - j))

    def queries_out(g):
        dq = query_grad(g + 1).reshape(4, 64, HD)
        dq_own[g] = dq
        dq_st[g] = dq.astype(BF)
        for j in (2, 1, 3):
            send(dq_st.at[g, (u + 4 - j) % 4], dq_in.at[j - 1, g], dq_s, dq_r.at[g], shift(4 - j))

    for g in FAR[:2]:
        for qc in range(5):
            probs(g + 1, qc)
        keys_out(g)
    for qc in range(5):
        probs(0, qc)
    dk, dv = key_grad(0), value_grad(0)
    dkvt_own[0] = dk[0:32]
    dkvt_own[1] = dv[0:32]
    for j in (2, 1, 3):
        part = slice(j * 32, j * 32 + 32)
        dkvt_st[j - 1, 0] = dk[part].astype(BF)
        dkvt_st[j - 1, 1] = dv[part].astype(BF)
        send(dkvt_st.at[j - 1], dkvt_in.at[j - 1], dkvt_s, dkvt_r, turn(4 - j))
    for g in FAR[2:]:
        probs(g + 1, 0)
    dq_text[...] = query_grad(0)
    for j in (2, 1, 3):
        dqt_st[j - 1] = dq_text[text_part(j)].astype(BF)
        send(dqt_st.at[j - 1], dqt_in.at[j - 1], dqt_s, dqt_r, shift(4 - j))
    for g in FAR[2:]:
        for qc in range(1, 5):
            probs(g + 1, qc)
        keys_out(g)
    for g in FAR:
        queries_out(g)

    def plus(own_term, terms):
        for t in terms:
            own_term = own_term + t.astype(F32)
        return own_term

    def hand_back(g, part):
        for i in range(4 * g, 4 * g + 4):
            if i:
                at, n = (0, 1) if part else (1, 2)
                rows = pl.ds(at, n)
                send(out_st.at[i, rows], fin.at[head, rows], p4_s, p4_r, column(i, 1))

    def keys_back(g):
        slots = pl.ds(4 * g, 4)
        arrive(dkv_in.at[:, g], dkv_r.at[g])
        for n in (0, 1):
            total = plus(dkv_own[g, n], [dkv_in[j, g, n] for j in range(3)])
            out_st[slots, n + 1] = total.astype(BF).reshape(4, 16, HD)
        hand_back(g, 0)

    def queries_back(g):
        slots = pl.ds(4 * g, 4)
        arrive(dq_in.at[:, g], dq_r.at[g])
        total = plus(dq_own[g, u], [dq_in[j, g] for j in range(3)])
        out_st[slots, 0] = total.astype(BF).reshape(4, 16, HD)
        hand_back(g, 1)

    keys_back(FAR[0])
    keys_back(FAR[1])
    arrive(dqt_in, dqt_r)
    arrive(dkvt_in, dkvt_r)

    tout[0] = plus(dq_text[text_part(0)], [dqt_in[j] for j in range(3)]).astype(BF)
    tout[1] = plus(dkvt_own[0], [dkvt_in[j, 0] for j in range(3)]).astype(BF)
    tout[2] = plus(dkvt_own[1], [dkvt_in[j, 1] for j in range(3)]).astype(BF)
    tcopy = pltpu.make_async_remote_copy(
        tout, tfin, tx_s, tx_r, device_id=partner, device_id_type=MESH)

    @pl.when(y != zh)
    def _():
        tcopy.start()

    @pl.when(y == zh)
    def _():
        tfin[...] = tout[...]

    keys_back(FAR[2])
    queries_back(FAR[0])
    keys_back(FAR[3])
    queries_back(FAR[1])
    queries_back(FAR[2])
    queries_back(FAR[3])
    fin[head] = out_st[0]

    arrive(own.at[pl.ds(0, 15)], p1_s)
    arrive(kv, kv_s)
    arrive(kv, qg_s)
    arrive(st_in, st_s)
    arrive(dkv_st, dkv_s)
    arrive(dq_in, dq_s)
    arrive(dkvt_st, dkvt_s)
    arrive(dqt_st, dqt_s)
    arrive(fin.at[pl.ds(0, 15)], p4_s)
    arrive(fin.at[pl.ds(0, 15)], p4_r)

    @pl.when(y != zh)
    def _():
        tcopy.wait()


def widen(fin, tfin, oq, ok, ov, otq, otk, otv):
    for n, out in enumerate((oq, ok, ov)):
        for h in range(16):
            out[:, h * HD:(h + 1) * HD] = fin[h, n].astype(F32)
    for n, out in enumerate((otq, otk, otv)):
        out[...] = tfin[n].astype(F32)


def per_device(*args):
    hbm = pl.BlockSpec(memory_space=pltpu.HBM)
    vmem = pl.BlockSpec(memory_space=pltpu.VMEM)
    sem = pltpu.SemaphoreType.DMA
    V = pltpu.VMEM
    landed = pl.pallas_call(
        body,
        out_shape=[pltpu.VMEM((16, 3, 16, HD), BF), pltpu.VMEM((3, 32, HD), BF)],
        in_specs=[hbm] * 8,
        out_specs=[vmem] * 2,
        scratch_shapes=[
            V((4, 16, 2048), BF), V((16, 4, 16, HD), BF), V((16, 4, 16, HD), BF),
            V((4, 16, 2, 16, HD), BF), V((3, 16, 2, 16, HD), BF), V((4, 128, HD), BF),
            V((ROWS, HD), BF), V((ROWS, HD), BF), V((ROWS, HD), BF), V((ROWS, HD), BF), V((HD, ROWS), BF),
            V((5, ROWS, 256), F32), V((5, ROWS, 256), F32), V((ROWS, ROWS), BF), V((ROWS, ROWS), BF),
            V((5, 8, 256), F32), V((5, 8, 256), F32), V((5, 8, 256), F32), V((32, HD), F32), V((3, 32, HD), F32),
            V((3, 4, 2, 64, HD), BF), V((3, 4, 2, 64, HD), BF), V((4, 2, 64, HD), F32),
            V((3, 2, 32, HD), BF), V((3, 2, 32, HD), BF), V((2, 32, HD), F32),
            V((4, 4, 64, HD), BF), V((3, 4, 64, HD), BF), V((4, 4, 64, HD), F32),
            V((3, 32, HD), BF), V((3, 32, HD), BF), V((HD, HD), F32),
            V((16, 3, 16, HD), BF), V((3, 32, HD), BF),
            sem, sem,
            sem, sem((15,)), sem, sem, sem((4,)), sem, sem,
            sem, sem((4,)), sem, sem, sem, sem((4,)), sem, sem,
            sem, sem, sem, sem,
        ],
        compiler_params=pltpu.CompilerParams(
            collective_id=0, has_side_effects=True, vmem_limit_bytes=48 * 1024 * 1024),
        cost_estimate=pl.CostEstimate(flops=1_700_000_000, bytes_accessed=2_000_000, transcendentals=1_300_000),
    )(*[pltpu.with_memory_space_constraint(a, pltpu.HBM) for a in args])
    return pl.pallas_call(
        widen,
        out_shape=[jax.ShapeDtypeStruct((16, 2048), F32)] * 3 + [jax.ShapeDtypeStruct((32, HD), F32)] * 3,
        in_specs=[vmem] * 2,
        out_specs=[vmem] * 6,
        compiler_params=pltpu.CompilerParams(vmem_limit_bytes=4 * 1024 * 1024),
    )(*landed)


def solution(mesh):
    tokens = P(("seq", "mlp"), None)
    return jax.shard_map(
        per_device,
        mesh=mesh,
        in_specs=(P(), P(), P(), P(), tokens, tokens, tokens, tokens),
        out_specs=(tokens, tokens, tokens, P("mlp", "seq"), P("mlp", "seq"), P("mlp", "seq")),
        check_vma=False,
    )
```

```python
import jax
import jax.numpy as jnp
from jax import lax
from jax.experimental import pallas as pl
from jax.experimental.pallas import tpu as pltpu
from jax.sharding import PartitionSpec as P

HD = 128
LOG2E = 1.4426950408889634
SCALE = HD ** -0.5
UNIT = SCALE * LOG2E
BF = jnp.bfloat16
F32 = jnp.float32
MESH = pl.DeviceIdType.MESH

SLOTS = ((0, 0), (0, 1), (1, 0), (7, 0), (1, 1), (7, 1), (2, 0), (6, 0),
         (2, 1), (6, 1), (3, 0), (5, 0), (3, 1), (5, 1), (4, 0), (4, 1))

START = (0, 128, 384, 640, 896)
SIZE = (128, 256, 256, 256, 256)
ROWS = 1152


def nt(a, b):
    return lax.dot_general(a, b, (((1,), (1,)), ((), ())), preferred_element_type=F32)


def nn(a, b):
    return lax.dot_general(a, b, (((1,), (0,)), ((), ())), preferred_element_type=F32)


def body(
    tq, tk, tv, tg, iq, ik, iv, ig,
    fin, tfin,
    flat, stage, own, qg, kv, text,
    qall, kall, vall, gall, ktall,
    e_buf, dp_buf, pb_buf, ds_buf, mx, sm, dl, st, st_in,
    dkv_st, dkv_in, dkv_own, dkvt_st, dkvt_in, dkvt_own,
    dq_st, dq_in, dq_own, dqt_st, dqt_in, dq_text,
    out_st, tout,
    in_sem, text_sem,
    p1_s, p1_r, qg_s, kv_s, p2_r, st_s, st_r,
    dkv_s, dkv_r, dkvt_s, dkvt_r, dq_s, dq_r, dqt_s, dqt_r,
    p4_s, p4_r, tx_s, tx_r,
):
    seq = lax.axis_index("seq")
    mlp = lax.axis_index("mlp")
    z0, y, core = seq // 8, (seq // 2) % 4, seq % 2
    x, zh = mlp // 4, mlp % 4
    z = zh * 2 + z0

    head = z0 * 8 + zh * 2 + core
    u = x * (1 - core) + y * core
    v = y * (1 - core) + x * core

    def along(jx, jy):
        return {"seq": z0 * 8 + ((y + jy) % 4) * 2 + core, "mlp": ((x + jx) % 4) * 4 + zh}

    def shift(j):
        return along(j * (1 - core), j * core)

    def turn(j):
        return along(j * core, j * (1 - core))

    def block(a, b):
        return a * (4 - 3 * core) + b * (1 + 3 * core)

    def around(i, sign):
        dz, dc = SLOTS[i]
        there = (z + sign * dz + 8) % 8
        other = 1 - core if dc else core
        return there % 2, there // 2, other

    def column(i, sign):
        zo, zi, other = around(i, sign)
        return {"seq": zo * 8 + y * 2 + other, "mlp": x * 4 + zi}

    def head_of(i, sign):
        zo, zi, other = around(i, sign)
        return zo * 8 + zi * 2 + other

    partner = {"seq": z0 * 8 + zh * 2 + core, "mlp": x * 4 + y}
    def send(src, dst, ss, rs, to):
        pltpu.make_async_remote_copy(src, dst, ss, rs, device_id=to, device_id_type=MESH).start()

    def arrive(ref, sem):
        pltpu.make_async_copy(ref, ref, sem).wait()

    for n, ref in enumerate((iq, ig, ik, iv)):
        pltpu.make_async_copy(ref, flat.at[n], in_sem).start()

    barrier = pltpu.get_barrier_semaphore()
    def greet(to):
        pl.semaphore_signal(barrier, inc=1, device_id=to, device_id_type=MESH)

    for i in range(15, 0, -1):
        greet(column(i, 1))

    for j in (2, 3, 1):
        greet(turn(j))
        greet(shift(j))

    col = pl.ds(pl.multiple_of(head * HD, HD), HD)
    for n, ref in enumerate((tq, tg, tk, tv)):
        for j in range(4):
            owner = block(j, v) if n < 2 else block(u, (v + 4 - j) % 4)
            rows = pl.ds(pl.multiple_of(owner * 32, 32), 32)
            pltpu.make_async_copy(ref.at[rows, col], text.at[n, pl.ds(j * 32, 32)], text_sem).start()

    arrive(flat, in_sem)
    for n in range(4):
        for h in range(16):
            stage[h, n] = flat[n, :, h * HD:(h + 1) * HD]

    pl.semaphore_wait(barrier, 21)

    for i in range(1, 16):
        send(stage.at[head_of(i, -1)], own.at[i], p1_s, p1_r.at[i - 1], column(i, -1))
    own[0] = stage[head]

    for i in range(16):
        if i:
            arrive(own.at[i], p1_r.at[i - 1])
        g = i // 4
        for j in (2, 1, 3):
            send(own.at[i, pl.ds(2, 2)], kv.at[j - 1, i], kv_s, p2_r.at[g], turn(j))
            send(own.at[i, pl.ds(0, 2)], qg.at[u, i], qg_s, p2_r.at[g], shift(j))

    def query_rows(qc):
        return pl.ds(START[qc], SIZE[qc])

    def width(qc):
        return 128 if qc == 0 else 256

    def key_rows(kc):
        return pl.ds(START[kc], SIZE[kc])

    def pass_one(kc, qc):
        kr, qr, n = key_rows(kc), query_rows(qc), pl.ds(0, width(qc))
        scores = nt(kall[kr], qall[qr])
        top = jnp.max(scores, axis=0, keepdims=True)
        e = jnp.exp2((scores - top) * UNIT)
        dp = nt(vall[kr], gall[qr])
        mx[qc, kc:kc + 1, n] = top
        sm[qc, kc:kc + 1, n] = jnp.sum(e, axis=0, keepdims=True)
        dl[qc, kc:kc + 1, n] = jnp.sum(e * dp, axis=0, keepdims=True)
        e_buf[qc, kr, n] = e
        dp_buf[qc, kr, n] = dp

    def take(g):
        slots = pl.ds(4 * g, 4)
        arrive(own.at[pl.ds(0, 12)], p2_r.at[g])
        qg[u, slots] = own[slots, 0:2]
        for b in range(4):
            r = pl.ds(START[g + 1] + 64 * b, 64)
            k, val = (kv[b - 1, slots, 0], kv[b - 1, slots, 1]) if b else (own[slots, 2], own[slots, 3])
            kall[r] = k.reshape(64, HD)
            vall[r] = val.reshape(64, HD)
            qall[r] = qg[b, slots, 0].reshape(64, HD)
            gall[r] = qg[b, slots, 1].reshape(64, HD)

    arrive(text, text_sem)
    qall[0:128] = text[0]
    gall[0:128] = text[1]
    kall[0:128] = text[2]
    vall[0:128] = text[3]
    pass_one(0, 0)
    for g in range(4):
        take(g)
        for c in range(g + 1):
            pass_one(g + 1, c)
            pass_one(c, g + 1)
        if g < 3:
            pass_one(g + 1, g + 1)

    for qc in range(5):
        if qc == 4:
            pass_one(4, 4)
        n = pl.ds(0, width(qc))
        top = jnp.max(mx[qc, 0:5, n], axis=0, keepdims=True)
        w = jnp.exp2((mx[qc, 0:5, n] - top) * UNIT)
        total = jnp.sum(w * sm[qc, 0:5, n], axis=0, keepdims=True)
        dsum = jnp.sum(w * dl[qc, 0:5, n], axis=0, keepdims=True)
        for i, row in enumerate((top, total, dsum)):
            for half in range(1 if qc == 0 else 2):
                b = 2 * qc - 1 + half if qc else 0
                st[i * 9 + b:i * 9 + b + 1] = row[:, half * 128:(half + 1) * 128]
    for j in (2, 3, 1):
        send(st, st_in.at[j - 1], st_s, st_r, shift(j))
    ktall[...] = kall[...].T
    arrive(st_in, st_r)

    tops, sums, dsums = ([st[n:n + 9]] + [st_in[j, n:n + 9] for j in range(3)] for n in (0, 9, 18))
    gtop = jnp.maximum(jnp.maximum(tops[0], tops[1]), jnp.maximum(tops[2], tops[3]))
    ws = [jnp.exp2((t - gtop) * UNIT) for t in tops]
    gsum = sum(w * t for w, t in zip(ws, sums))
    gd = sum(w * t for w, t in zip(ws, dsums))
    inv = 1.0 / gsum

    delta = gd * inv

    def as_row(a, qc):
        if qc == 0:
            return a[0:1]
        return jnp.concatenate([a[2 * qc - 1:2 * qc], a[2 * qc:2 * qc + 1]], axis=1)

    for qc in range(5):
        n = pl.ds(0, width(qc))
        mx[qc, 0:5, n] = jnp.exp2((mx[qc, 0:5, n] - as_row(gtop, qc)) * UNIT) * as_row(inv, qc)
        dl[qc, 0:1, n] = as_row(delta, qc)

    def probs(kc, qc):
        kr, qr, n = key_rows(kc), query_rows(qc), pl.ds(0, width(qc))
        p = e_buf[qc, kr, n] * mx[qc, kc:kc + 1, n]
        pb_buf[kr, qr] = p.astype(BF)
        ds_buf[kr, qr] = (p * (dp_buf[qc, kr, n] - dl[qc, 0:1, n])).astype(BF)

    def value_grad(kc):
        return nn(pb_buf[key_rows(kc)], gall[...])

    def key_grad(kc):
        return nn(ds_buf[key_rows(kc)], qall[...]) * SCALE

    def query_grad(qc):
        return (nn(ktall[...], ds_buf[:, query_rows(qc)]) * SCALE).T

    def text_part(j):
        return pl.ds(pl.multiple_of(((u + 4 - j) % 4) * 32, 32), 32)

    FAR = (3, 2, 1, 0)

    def keys_out(g):
        dk, dv = key_grad(g + 1), value_grad(g + 1)
        dkv_own[g, 0] = dk[0:64]
        dkv_own[g, 1] = dv[0:64]
        for j in (2, 1, 3):
            dkv_st[j - 1, g, 0] = dk[64 * j:64 * j + 64].astype(BF)
            dkv_st[j - 1, g, 1] = dv[64 * j:64 * j + 64].astype(BF)
            send(dkv_st.at[j - 1, g], dkv_in.at[j - 1, g], dkv_s, dkv_r.at[g], turn(4 - j))

    def queries_out(g):
        dq = query_grad(g + 1).reshape(4, 64, HD)
        dq_own[g] = dq
        dq_st[g] = dq.astype(BF)
        for j in (2, 1, 3):
            send(dq_st.at[g, (u + 4 - j) % 4], dq_in.at[j - 1, g], dq_s, dq_r.at[g], shift(4 - j))

    for g in FAR[:1]:
        for qc in range(5):
            probs(g + 1, qc)
        keys_out(g)
    for qc in range(5):
        probs(0, qc)
    dk, dv = key_grad(0), value_grad(0)
    dkvt_own[0] = dk[0:32]
    dkvt_own[1] = dv[0:32]
    for j in (2, 1, 3):
        part = slice(j * 32, j * 32 + 32)
        dkvt_st[j - 1, 0] = dk[part].astype(BF)
        dkvt_st[j - 1, 1] = dv[part].astype(BF)
        send(dkvt_st.at[j - 1], dkvt_in.at[j - 1], dkvt_s, dkvt_r, turn(4 - j))
    for g in FAR[1:]:
        probs(g + 1, 0)
    dq_text[...] = query_grad(0)
    for j in (2, 1, 3):
        dqt_st[j - 1] = dq_text[text_part(j)].astype(BF)
        send(dqt_st.at[j - 1], dqt_in.at[j - 1], dqt_s, dqt_r, shift(4 - j))
    for g in FAR[1:]:
        for qc in range(1, 5):
            probs(g + 1, qc)
        keys_out(g)
    for g in FAR:
        queries_out(g)

    def plus(own_term, terms):
        for t in terms:
            own_term = own_term + t.astype(F32)
        return own_term

    def hand_back(g, part):
        for i in range(4 * g, 4 * g + 4):
            if i:
                at, n = (0, 1) if part else (1, 2)
                rows = pl.ds(at, n)
                send(out_st.at[i, rows], fin.at[head, rows], p4_s, p4_r, column(i, 1))

    def keys_back(g):
        slots = pl.ds(4 * g, 4)
        arrive(dkv_in.at[:, g], dkv_r.at[g])
        for n in (0, 1):
            total = plus(dkv_own[g, n], [dkv_in[j, g, n] for j in range(3)])
            out_st[slots, n + 1] = total.astype(BF).reshape(4, 16, HD)
        hand_back(g, 0)

    def queries_back(g):
        slots = pl.ds(4 * g, 4)
        arrive(dq_in.at[:, g], dq_r.at[g])
        total = plus(dq_own[g, u], [dq_in[j, g] for j in range(3)])
        out_st[slots, 0] = total.astype(BF).reshape(4, 16, HD)
        hand_back(g, 1)

    arrive(dqt_in, dqt_r)
    arrive(dkvt_in, dkvt_r)

    tout[0] = plus(dq_text[text_part(0)], [dqt_in[j] for j in range(3)]).astype(BF)
    tout[1] = plus(dkvt_own[0], [dkvt_in[j, 0] for j in range(3)]).astype(BF)
    tout[2] = plus(dkvt_own[1], [dkvt_in[j, 1] for j in range(3)]).astype(BF)
    tcopy = pltpu.make_async_remote_copy(
        tout, tfin, tx_s, tx_r, device_id=partner, device_id_type=MESH)

    @pl.when(y != zh)
    def _():
        tcopy.start()

    @pl.when(y == zh)
    def _():
        tfin[...] = tout[...]

    keys_back(FAR[0])
    keys_back(FAR[1])
    keys_back(FAR[2])
    queries_back(FAR[0])
    keys_back(FAR[3])
    queries_back(FAR[1])
    queries_back(FAR[2])
    queries_back(FAR[3])
    fin[head] = out_st[0]

    arrive(own.at[pl.ds(0, 15)], p1_s)
    arrive(kv, kv_s)
    arrive(kv, qg_s)
    arrive(st_in, st_s)
    arrive(dkv_st, dkv_s)
    arrive(dq_in, dq_s)
    arrive(dkvt_st, dkvt_s)
    arrive(dqt_st, dqt_s)
    arrive(fin.at[pl.ds(0, 15)], p4_s)
    arrive(fin.at[pl.ds(0, 15)], p4_r)

    @pl.when(y != zh)
    def _():
        tcopy.wait()


def widen(fin, tfin, oq, ok, ov, otq, otk, otv):
    for n, out in enumerate((oq, ok, ov)):
        for h in range(16):
            out[:, h * HD:(h + 1) * HD] = fin[h, n].astype(F32)
    for n, out in enumerate((otq, otk, otv)):
        out[...] = tfin[n].astype(F32)


def per_device(*args):
    hbm = pl.BlockSpec(memory_space=pltpu.HBM)
    vmem = pl.BlockSpec(memory_space=pltpu.VMEM)
    sem = pltpu.SemaphoreType.DMA
    V = pltpu.VMEM
    landed = pl.pallas_call(
        body,
        out_shape=[pltpu.VMEM((16, 3, 16, HD), BF), pltpu.VMEM((3, 32, HD), BF)],
        in_specs=[hbm] * 8,
        out_specs=[vmem] * 2,
        scratch_shapes=[
            V((4, 16, 2048), BF), V((16, 4, 16, HD), BF), V((16, 4, 16, HD), BF),
            V((4, 16, 2, 16, HD), BF), V((3, 16, 2, 16, HD), BF), V((4, 128, HD), BF),
            V((ROWS, HD), BF), V((ROWS, HD), BF), V((ROWS, HD), BF), V((ROWS, HD), BF), V((HD, ROWS), BF),
            V((5, ROWS, 256), F32), V((5, ROWS, 256), F32), V((ROWS, ROWS), BF), V((ROWS, ROWS), BF),
            V((5, 8, 256), F32), V((5, 8, 256), F32), V((5, 8, 256), F32), V((32, HD), F32), V((3, 32, HD), F32),
            V((3, 4, 2, 64, HD), BF), V((3, 4, 2, 64, HD), BF), V((4, 2, 64, HD), F32),
            V((3, 2, 32, HD), BF), V((3, 2, 32, HD), BF), V((2, 32, HD), F32),
            V((4, 4, 64, HD), BF), V((3, 4, 64, HD), BF), V((4, 4, 64, HD), F32),
            V((3, 32, HD), BF), V((3, 32, HD), BF), V((HD, HD), F32),
            V((16, 3, 16, HD), BF), V((3, 32, HD), BF),
            sem, sem,
            sem, sem((15,)), sem, sem, sem((4,)), sem, sem,
            sem, sem((4,)), sem, sem, sem, sem((4,)), sem, sem,
            sem, sem, sem, sem,
        ],
        compiler_params=pltpu.CompilerParams(
            collective_id=0, has_side_effects=True, vmem_limit_bytes=48 * 1024 * 1024),
        cost_estimate=pl.CostEstimate(flops=1_700_000_000, bytes_accessed=2_000_000, transcendentals=1_300_000),
    )(*[pltpu.with_memory_space_constraint(a, pltpu.HBM) for a in args])
    return pl.pallas_call(
        widen,
        out_shape=[jax.ShapeDtypeStruct((16, 2048), F32)] * 3 + [jax.ShapeDtypeStruct((32, HD), F32)] * 3,
        in_specs=[vmem] * 2,
        out_specs=[vmem] * 6,
        compiler_params=pltpu.CompilerParams(vmem_limit_bytes=4 * 1024 * 1024),
    )(*landed)


def solution(mesh):
    tokens = P(("seq", "mlp"), None)
    return jax.shard_map(
        per_device,
        mesh=mesh,
        in_specs=(P(), P(), P(), P(), tokens, tokens, tokens, tokens),
        out_specs=(tokens, tokens, tokens, P("mlp", "seq"), P("mlp", "seq"), P("mlp", "seq")),
        check_vma=False,
    )
```
